256 devices in a mesh: ctx: 32 (over z, x_hi, core), tp: 8 (over y, x_lo).
Axes of the slice: x: 4 (x_hi: 2, x_lo: 2; x = x_hi * 2 + x_lo), y: 4, z: 8, core: 2. Of those that a mesh axis runs over, the one named last changes fastest.
Arguments:
- query_in: bfloat16 [4096, 8192], P('ctx', 'tp'), may hold values from -6 to 6
- key_in: bfloat16 [4096, 8192], P('ctx', 'tp'), may hold values from -6 to 6
- value_in: bfloat16 [4096, 8192], P('ctx', 'tp'), may hold values from -6 to 6
- short_query: float32 [3, 8192], P(None, 'tp'), may hold values from -3 to 3
- short_key: float32 [3, 8192], P(None, 'tp'), may hold values from -3 to 3
- short_value: float32 [3, 8192], P(None, 'tp'), may hold values from -3 to 3
- long_filter: float32 [4096, 8192], P('ctx', 'tp'), may hold values from -0.09375 to 0.09375
- skip_gain: float32 [8192], P('tp'), may hold values from 0.5 to 1.5
- out_weight: bfloat16 [8192, 4096], P('tp', 'ctx'), may hold values from -0.125 to 0.125
- cotangent: bfloat16 [4096, 4096], P('ctx', 'tp'), may hold values from -4 to 4
Outputs:
- mixed_out: bfloat16 [4096, 4096], P('ctx', 'tp')
- grad_query: bfloat16 [4096, 8192], P('ctx', 'tp')
- grad_key: bfloat16 [4096, 8192], P('ctx', 'tp')
- grad_value: bfloat16 [4096, 8192], P('ctx', 'tp')
- grad_filter: bfloat16 [4096, 8192], P('ctx', 'tp')
- grad_skip: float32 [8192], P('tp')
- grad_short: float32 [3, 3, 8192], P(None, None, 'tp')
The draws below stay inside these ranges and needn't reach their ends.
All inputs are finite; a program needn't handle non-finite values.
Results may differ from the reference program's by a relative error of at most 0.0049.
Values may be sent and summed in bfloat16 or wider, within the bound.
A program may use at most 128 MiB of HBM per device.

```python
import math
import jax
import jax.numpy as jnp
from jax import lax

CH = 8192
D_OUT = 4096
TAPS = 3
TOKENS = 4096


def with_spikes(values, key, source, target, blocks, factor):
    owner, partner = [(jnp.arange(values.shape[dim]) // (values.shape[dim] // blocks)).reshape([-1 if axis == dim else 1 for axis in range(values.ndim)]) for dim in (source, target)]
    chosen = jax.random.permutation(key, blocks)[partner]
    strong = (owner == chosen) | (owner == (partner + blocks // 2) % blocks)
    return jnp.where(strong, factor * values, values)


def block_scale(stream_key, shape, shards, low, top_value):
    factor_of = 1.0
    for dim, shards_of in shards:
        draws = jax.random.uniform(jax.random.fold_in(jax.random.fold_in(stream_key, 6), dim), (shards_of,), jnp.float32, low / len(shards), top_value / len(shards))
        factor_of = factor_of * jnp.repeat(jnp.exp(draws), shape[dim] // shards_of).reshape((-1,) + (1,) * (len(shape) - 1 - dim))
    return factor_of


def scatter_about(own_key, extent, scale, limit, shards=(), dtype=jnp.bfloat16):
    level = block_scale(own_key, extent, shards, -0.22, 0.18) if shards else 1.0
    values = jax.random.normal(own_key, extent, jnp.float32) * scale * level
    return jnp.minimum(jnp.maximum(values, -limit), limit).astype(dtype)


def heavy_noise(stream_key, shape, spread, bound, pieces, heavy, kind=jnp.bfloat16):
    drawn = spread * jax.random.normal(stream_key, shape, jnp.float32)
    if pieces:
        drawn = drawn * block_scale(stream_key, shape, pieces, -0.22, 0.18)
    return jnp.clip(with_spikes(drawn, jax.random.fold_in(stream_key, 3), *heavy), -bound, bound).astype(kind)


def setup_inputs(seed: int = 0) -> dict:
    keys = jax.random.split(jax.random.key(seed), 11)
    return {
        "query_in": scatter_about(keys[0], (TOKENS, CH), 1.0, 6.0, ((0, 32), (1, 8))),
        "key_in": scatter_about(keys[1], (TOKENS, CH), 1.0, 6.0, ((0, 32), (1, 8))),
        "value_in": scatter_about(keys[2], (TOKENS, CH), 1.0, 6.0, ((0, 32), (1, 8))),
        "short_query": scatter_about(keys[3], (TAPS, CH), 0.6, 3.0, ((1, 8),), jnp.float32),
        "short_key": scatter_about(keys[4], (TAPS, CH), 0.6, 3.0, ((1, 8),), jnp.float32),
        "short_value": scatter_about(keys[5], (TAPS, CH), 0.6, 3.0, ((1, 8),), jnp.float32),
        "long_filter": scatter_about(keys[6], (TOKENS, CH), TOKENS ** -0.5, 0.09375, ((0, 32), (1, 8)), jnp.float32),
        "skip_gain": jnp.clip(0.5 + 1.0 * jax.random.uniform(keys[7], (CH,), jnp.float32) ** block_scale(keys[7], (CH,), ((0, 8),), -0.2, 0.2), 0.5, 1.5),
        "out_weight": heavy_noise(keys[8], (CH, D_OUT), CH ** -0.5, 0.125, ((0, 8), (1, 32)), (0, 1, 32, 2.75)),
        "cotangent": scatter_about(keys[9], (TOKENS, D_OUT), 0.5, 4.0, ((0, 32), (1, 8))),
    }


def short_forward(signal, taps):
    length = signal.shape[0]
    padded = jnp.pad(signal, ((2, 0), (0, 0)))
    return taps[0] * signal + taps[1] * padded[1:length + 1] + taps[2] * padded[0:length]


def short_backward(grads, taps):
    length = grads.shape[0]
    padded = jnp.pad(grads, ((0, 2), (0, 0)))
    return taps[0] * grads + taps[1] * padded[1:length + 1] + taps[2] * padded[2:length + 2]


def short_taps(grads, signal):
    length = signal.shape[0]
    padded = jnp.pad(signal, ((2, 0), (0, 0)))
    return jnp.stack([jnp.sum(grads * padded[2 - offset:2 - offset + length], axis=0) for offset in range(3)])


def causal_conv(filt, signal):
    length = filt.shape[0]
    spec = jnp.fft.rfft(filt, n=2 * length, axis=0) * jnp.fft.rfft(signal, n=2 * length, axis=0)
    return jnp.fft.irfft(spec, n=2 * length, axis=0)[:length]


def adjoint_conv(filt, signal):
    length = filt.shape[0]
    spec = jnp.conj(jnp.fft.rfft(filt, n=2 * length, axis=0)) * jnp.fft.rfft(signal, n=2 * length, axis=0)
    return jnp.fft.irfft(spec, n=2 * length, axis=0)[:length]


def by_blocks(func, first, second):
    length, channels = first.shape
    block_size = math.gcd(channels, 512)
    block_count = channels // block_size
    leading = jnp.moveaxis(first.reshape(length, block_count, block_size), 1, 0)
    trailing = jnp.moveaxis(second.reshape(length, block_count, block_size), 1, 0)
    result = lax.map(lambda operands: func(operands[0], operands[1]), (leading, trailing))
    return jnp.moveaxis(result, 0, 1).reshape(length, channels)


def reference(query_in, key_in, value_in, short_query, short_key, short_value, long_filter, skip_gain, out_weight, cotangent):
    query_f = query_in.astype(jnp.float32)
    key_f = key_in.astype(jnp.float32)
    value_f = value_in.astype(jnp.float32)
    q_short = short_forward(query_f, short_query)
    k_short = short_forward(key_f, short_key)
    v_short = short_forward(value_f, short_value)
    gated = k_short * v_short
    mixing = by_blocks(causal_conv, long_filter, gated) + skip_gain * gated
    hidden = (q_short * mixing).astype(jnp.bfloat16)
    mixed_out = jnp.dot(hidden, out_weight, preferred_element_type=jnp.float32).astype(jnp.bfloat16)
    grad_hidden = jnp.dot(cotangent, out_weight.T, preferred_element_type=jnp.float32)
    grad_qs = grad_hidden * mixing
    grad_mix = grad_hidden * q_short
    grad_gated = by_blocks(adjoint_conv, long_filter, grad_mix) + skip_gain * grad_mix
    grad_filter = by_blocks(adjoint_conv, gated, grad_mix).astype(jnp.bfloat16)
    grad_skip = jnp.sum(grad_mix * gated, axis=0)
    grad_ks = grad_gated * v_short
    grad_vs = grad_gated * k_short
    grad_query = short_backward(grad_qs, short_query).astype(jnp.bfloat16)
    grad_key = short_backward(grad_ks, short_key).astype(jnp.bfloat16)
    grad_value = short_backward(grad_vs, short_value).astype(jnp.bfloat16)
    grad_short = jnp.stack([short_taps(grad_qs, query_f), short_taps(grad_ks, key_f), short_taps(grad_vs, value_f)])
    return mixed_out, grad_query, grad_key, grad_value, grad_filter, grad_skip, grad_short
```

```python
import jax
import jax.numpy as jnp
import ml_dtypes
import numpy as np
from jax import lax
from jax.experimental import pallas as pl
from jax.experimental.pallas import tpu as pltpu
from jax.sharding import PartitionSpec as P

F32 = jnp.float32
BF16 = jnp.bfloat16
GROUP = 16
FILTER, GATED, MIXING, GRAD_MIX, GRAD_GATED, GRAD_FILTER = range(6)


def halves(matrix):
    high = matrix.astype(np.float32).astype(ml_dtypes.bfloat16)
    low = (matrix - high.astype(np.float64)).astype(np.float32).astype(ml_dtypes.bfloat16)
    return np.stack([high, low])


def tables(n, seq):
    total = 2 * n * seq
    q = np.arange(n + 1)
    m = np.arange(n)
    theta = 2 * np.pi * ((q[:, None] * m[None, :]) % (2 * n)) / (2 * n)
    forward = np.concatenate([np.cos(theta), -np.sin(theta)[1:n]])
    weight = np.where((q == 0) | (q == n), 1.0, 2.0)[:, None] / total
    back = np.concatenate([weight * np.cos(theta), (-weight * np.sin(theta))[1:n]]).T
    eye = np.eye(GROUP)
    j = np.arange(seq)
    phi = 2 * np.pi * ((j[:, None] * j[None, :]) % seq) / seq
    c, s = np.cos(phi), np.sin(phi)
    inner = np.block([[c, -s], [s, c]])
    inner_back = np.block([[c, s], [-s, c]])
    turn = 2 * np.pi * (q[:, None] * j[None, :]) / total
    twiddle = np.stack([np.cos(turn), np.sin(turn)]).astype(np.float32)
    twiddle = np.repeat(twiddle, GROUP, axis=1)
    return (
        halves(np.kron(forward, eye)),
        halves(np.kron(back, eye)),
        halves(np.stack([inner, inner_back])),
        twiddle,
    )


def split(value):
    high = value.astype(BF16)
    return high, (value - high.astype(F32)).astype(BF16)


def mm(left, right):
    return jnp.dot(left, right, preferred_element_type=F32)


def body(n, nz, ny, refs):
    (
        query, key, value, tap_q, tap_k, tap_v, filt, skip, weight, cot,
        outer_hbm, outer_back_hbm, inner_hbm, twiddle_hbm,
        mixed_out, out_q, out_k, out_v, out_filter, out_skip, out_short,
        outer, outer_back, inner, twiddle,
        halo, ext, short, gated, mixing, grad_hidden, grad_mix, gext,
        sent, got, wide, cots, part, part_b, core_got, chip_sent, chip_got, hid,
        rows_b, rows_got, pair_sent, pair_got, final_b,
        spec_u, spec_h, spec_d, stage, tails, tails_got, tails_sum,
        const_sem, a2a_send, a2a_recv, send, recv,
    ) = refs
    seq, ch = query.shape
    half = ch // 2
    rows = 16 * n
    q_rows = GROUP * (n + 1)
    me = lax.axis_index("ctx")
    tp = lax.axis_index("tp")
    z, b = lax.div(me, 4), lax.rem(me, 4)
    xh, core = lax.div(b, 2), lax.rem(b, 2)
    y, xl = lax.div(tp, 2), lax.rem(tp, 2)
    counter = [0]
    pending = []

    def remote(src, dst, ctx, t):
        k = counter[0]
        counter[0] += 1
        copy = pltpu.make_async_remote_copy(
            src_ref=src, dst_ref=dst, send_sem=send.at[k], recv_sem=recv.at[k],
            device_id=(ctx, t), device_id_type=pl.DeviceIdType.MESH,
        )
        copy.start()
        pending.append(copy)
        return copy

    def at16(index):
        return pl.ds(pl.multiple_of(index * 16, 16), 16)

    def lanes(index, size=128):
        return pl.ds(pl.multiple_of(index * size, 128), size)

    def block(index, size=None):
        size = seq if size is None else size
        return pl.ds(pl.multiple_of(index * size, size), size)

    def spread(k):
        def step(r, carry):
            dst = lax.rem(me + r, n)
            pltpu.make_async_remote_copy(
                src_ref=sent.at[k, at16(dst)], dst_ref=got.at[k, at16(me)],
                send_sem=a2a_send.at[k], recv_sem=a2a_recv.at[k],
                device_id=(dst, tp), device_id_type=pl.DeviceIdType.MESH,
            ).start()
            return carry

        lax.fori_loop(1, n, step, 0)
        got[k, at16(me), :] = sent[k, at16(me), :]

    def arrive(k):
        whole = got.at[k, pl.ds(0, rows - 16)]
        pltpu.make_async_copy(whole, whole, a2a_recv.at[k]).wait()

    def left(k):
        whole = sent.at[k, pl.ds(0, rows - 16)]
        pltpu.make_async_copy(whole, whole, a2a_send.at[k]).wait()

    def to_channels(x, k):
        for g in range(2):
            sent[k, :, g * seq : (g + 1) * seq] = x[:, g * half : (g + 1) * half].T.astype(BF16)

    def to_tokens(k):
        return jnp.concatenate(
            [got[k, :, g * seq : (g + 1) * seq].astype(F32).T for g in range(2)], axis=1
        )

    def forward(k, spec):
        u = got[k]
        stage[...] = mm(outer[0], u) + mm(outer[1], u)
        cos, sin = twiddle[0], twiddle[1]
        zero = jnp.zeros((GROUP, seq), F32)
        for g in range(2):
            cols = pl.ds(g * seq, seq)
            real = stage[:q_rows, cols]
            imag = jnp.concatenate([zero, stage[q_rows:, cols], zero])
            pair = jnp.concatenate([real * cos + imag * sin, imag * cos - real * sin], axis=1)
            high, low = split(pair)
            spec[g] = mm(high, inner[0, 0]) + mm(low, inner[0, 0]) + mm(high, inner[1, 0])

    def product(first, second, g, conj):
        ar, ai = first[g, :, :seq], first[g, :, seq:]
        br, bi = second[g, :, :seq], second[g, :, seq:]
        if conj:
            return jnp.concatenate([ar * br + ai * bi, ar * bi - ai * br], axis=1)
        return jnp.concatenate([ar * br - ai * bi, ar * bi + ai * br], axis=1)

    def inverse(first, second, conj, k):
        cos, sin = twiddle[0], twiddle[1]
        for g in range(2):
            high, low = split(product(first, second, g, conj))
            turned = mm(high, inner[0, 1]) + mm(low, inner[0, 1]) + mm(high, inner[1, 1])
            real, imag = turned[:, :seq], turned[:, seq:]
            cols = pl.ds(g * seq, seq)
            stage[:q_rows, cols] = real * cos - imag * sin
            stage[q_rows:, cols] = (imag * cos + real * sin)[GROUP : q_rows - GROUP]
        high, low = split(stage[...])
        result = mm(outer_back[0], high) + mm(outer_back[0], low) + mm(outer_back[1], high)
        sent[k] = result.astype(BF16)

    barrier = pltpu.get_barrier_semaphore()

    def greet(r, carry):
        pl.semaphore_signal(
            barrier, inc=1, device_id=(lax.rem(me + r, n), tp),
            device_id_type=pl.DeviceIdType.MESH,
        )
        return carry

    lax.fori_loop(1, n, greet, 0)
    others = [(y, 1 - xl)] + [(lax.rem(y + r, ny), xl) for r in range(1, ny)]
    for oy, ox in others:
        pl.semaphore_signal(
            barrier, inc=1, device_id=(me, oy * 2 + ox), device_id_type=pl.DeviceIdType.MESH
        )
    consts = [
        pltpu.make_async_copy(src, dst, const_sem.at[i])
        for i, (src, dst) in enumerate(
            [(outer_hbm, outer), (inner_hbm, inner), (twiddle_hbm, twiddle), (outer_back_hbm, outer_back)]
        )
    ]
    for copy in consts:
        copy.start()
    to_channels(filt[...], FILTER)
    wide[:, lanes(z)] = weight[...]
    cots[block(b), lanes(tp)] = cot[:, lanes(b)]
    tails[...] = jnp.zeros_like(tails)
    pl.semaphore_wait(barrier, n - 1 + len(others))

    following, preceding = lax.rem(me + 1, n), lax.rem(me + n - 1, n)
    halos = [
        remote(x.at[pl.ds(seq - 16, 16)], halo.at[i], following, tp)
        for i, x in enumerate((query, key, value))
    ]

    full = nz // 2 - 1
    up, down = lax.rem(z + 1, nz) * 4 + b, lax.rem(z + nz - 1, nz) * 4 + b

    def ring(s):
        if s < full:
            part_up = part_down = pl.ds(0, ch)
        else:
            part_up, part_down = pl.ds(0, half), pl.ds(half, half)
        slot_up, slot_down = lanes(lax.rem(z + nz - s, nz)), lanes(lax.rem(z + s, nz))
        if s == 0:
            src_up, src_down = weight.at[part_up], weight.at[part_down]
        else:
            src_up, src_down = wide.at[part_up, slot_up], wide.at[part_down, slot_down]
        return (
            remote(src_up, wide.at[part_up, slot_up], up, tp),
            remote(src_down, wide.at[part_down, slot_down], down, tp),
        )

    def landed(copies):
        for copy in copies:
            copy.wait_recv()

    def mate(r):
        other = lax.rem(b + r, 4)
        return other, z * 4 + other

    hop = ring(0)
    cot_first = []
    for r in range(1, 4):
        other, ctx = mate(r)
        cot_first.append(remote(cot.at[:, lanes(other)], cots.at[block(b), lanes(tp)], ctx, tp))
    spread(FILTER)

    landed(halos)
    taps = (tap_q, tap_k, tap_v)
    for i, x in enumerate((query, key, value)):
        ext[i, :8] = jnp.where(me == 0, 0.0, halo[i, 8:16].astype(F32))
        ext[i, 8:] = x[...].astype(F32)
        short[i] = (
            taps[i][0:1] * ext[i, pl.ds(8, seq)]
            + taps[i][1:2] * ext[i, pl.ds(7, seq)]
            + taps[i][2:3] * ext[i, pl.ds(6, seq)]
        )
    gated[...] = short[1] * short[2]
    to_channels(gated[...], GATED)
    spread(GATED)

    landed(cot_first)
    cot_pair = remote(cots.at[:, lanes(tp)], cots.at[:, lanes(tp)], me, y * 2 + 1 - xl)
    if full > 0:
        landed(hop)
        hop = ring(1)
    cot_pair.wait_recv()
    cot_last = []
    for oy, ox in others[1:]:
        cot_last.append(remote(cots.at[:, lanes(y, 256)], cots.at[:, lanes(y, 256)], me, oy * 2 + ox))

    for copy in consts:
        copy.wait()
    arrive(FILTER)
    forward(FILTER, spec_h)
    if full > 1:
        landed(hop)
        hop = ring(2)
    arrive(GATED)
    forward(GATED, spec_u)
    if full > 2:
        landed(hop)
        hop = ring(3)
    inverse(spec_h, spec_u, False, MIXING)
    spread(MIXING)

    landed(hop)
    landed(cot_last)

    def grad_columns(i, carry):
        part[:, lanes(i, 256)] = lax.dot_general(
            cots[...], wide[block(i, 256), :], (((1,), (1,)), ((), ())), preferred_element_type=F32
        )
        part_b[:, lanes(i, 256)] = part[:, lanes(i, 256)].astype(BF16)
        return carry

    lax.fori_loop(0, ch // 256, grad_columns, 0)
    sibling = z * 4 + xh * 2 + 1 - core
    twin = z * 4 + (1 - xh) * 2 + core
    core_copies = [
        remote(part_b.at[block(i * 2 + 1 - core)], core_got.at[i], sibling, tp) for i in range(2)
    ]

    arrive(MIXING)
    mixing[...] = to_tokens(MIXING) + skip[...] * gated[...]
    hid[block(b), :] = (short[0] * mixing[...]).astype(BF16)

    landed(core_copies)
    chip_sent[...] = (part[block((1 - xh) * 2 + core), :] + core_got[1 - xh].astype(F32)).astype(BF16)
    chip_copy = remote(chip_sent, chip_got, twin, tp)
    hid_twin = remote(hid.at[block(b)], hid.at[block(b)], twin, tp)
    hid_sib = remote(hid.at[block(b)], hid.at[block(b)], sibling, tp)

    chip_copy.wait_recv()
    grad_hidden[...] = (
        part[block(b), :] + core_got[xh].astype(F32) + chip_got[...].astype(F32)
    )
    grad_mix[...] = grad_hidden[...] * short[0]
    to_channels(grad_mix[...], GRAD_MIX)
    spread(GRAD_MIX)

    hid_twin.wait_recv()
    other_b = (1 - xh) * 2 + core
    hid_far = remote(hid.at[block(other_b)], hid.at[block(other_b)], sibling, tp)
    gext[0, :seq] = grad_hidden[...] * mixing[...]
    halo_q = remote(gext.at[0, pl.ds(0, 8)], gext.at[0, pl.ds(seq, 8)], preceding, tp)

    def tap_sums(i):
        grads = gext[i, :seq]
        for o in range(3):
            tails[8 * i + o, :] = jnp.sum(grads * ext[i, pl.ds(8 - o, seq)], axis=0)

    tap_sums(0)
    tails[24, :] = jnp.sum(grad_mix[...] * gated[...], axis=0)

    hid_sib.wait_recv()
    hid_far.wait_recv()

    def out_columns(i, carry):
        part[:, lanes(i, 256)] = mm(hid[...], wide[:, lanes(i, 256)])
        rows_b[:, lanes(i, 256)] = part[:, lanes(i, 256)].astype(BF16)
        return carry

    lax.fori_loop(0, wide.shape[1] // 256, out_columns, 0)
    rows_copies = [
        remote(rows_b.at[:, lanes(oy, 256)], rows_got.at[r], me, oy * 2 + ox)
        for r, (oy, ox) in enumerate(others[1:])
    ]

    arrive(GRAD_MIX)
    forward(GRAD_MIX, spec_d)
    inverse(spec_h, spec_d, True, GRAD_GATED)
    spread(GRAD_GATED)

    landed(rows_copies)
    total = part[:, lanes(y, 256)]
    for r in range(len(rows_copies)):
        total += rows_got[r].astype(F32)
    part[:, lanes(y, 256)] = total
    pair_sent[...] = part[:, lanes(y * 2 + 1 - xl)]
    pair_copy = remote(pair_sent, pair_got, me, y * 2 + 1 - xl)

    inverse(spec_u, spec_d, True, GRAD_FILTER)
    spread(GRAD_FILTER)

    pair_copy.wait_recv()
    final_b[...] = (part[:, lanes(tp)] + pair_got[...]).astype(BF16)
    mixed_out[:, lanes(b)] = final_b[block(b), :]
    final_copies = []
    for r in range(1, 4):
        other, ctx = mate(r)
        final_copies.append(remote(final_b.at[block(other)], mixed_out.at[:, lanes(b)], ctx, tp))

    def returned(i, out):
        gext[i, seq:] = jnp.where(me == n - 1, 0.0, gext[i, seq:])
        out[...] = (
            taps[i][0:1] * gext[i, pl.ds(0, seq)]
            + taps[i][1:2] * gext[i, pl.ds(1, seq)]
            + taps[i][2:3] * gext[i, pl.ds(2, seq)]
        ).astype(BF16)

    halo_q.wait_recv()
    returned(0, out_q)

    arrive(GRAD_GATED)
    grad = to_tokens(GRAD_GATED) + skip[...] * grad_mix[...]
    gext[1, :seq] = grad * short[2]
    gext[2, :seq] = grad * short[1]
    halo_kv = [
        remote(gext.at[i, pl.ds(0, 8)], gext.at[i, pl.ds(seq, 8)], preceding, tp) for i in (1, 2)
    ]
    tap_sums(1)
    tap_sums(2)

    across = ch // 128

    def tile(ref, d):
        return ref.at[block(lax.div(d, across), 8), lanes(lax.rem(d, across))]

    def hand_in(r, carry):
        dst = lax.rem(me + r, n)
        pltpu.make_async_remote_copy(
            src_ref=tile(tails, dst), dst_ref=tails_got.at[block(me, 8)],
            send_sem=a2a_send.at[6], recv_sem=a2a_recv.at[6],
            device_id=(dst, tp), device_id_type=pl.DeviceIdType.MESH,
        ).start()
        return carry

    def hand_out(r, carry):
        dst = lax.rem(me + r, n)
        pltpu.make_async_remote_copy(
            src_ref=tile(tails_sum, me), dst_ref=tile(tails_sum, me),
            send_sem=a2a_send.at[7], recv_sem=a2a_recv.at[7],
            device_id=(dst, tp), device_id_type=pl.DeviceIdType.MESH,
        ).start()
        return carry

    def tails_wait(sem):
        whole = tails_got.at[pl.ds(0, 8 * (n - 1))]
        pltpu.make_async_copy(whole, whole, sem).wait()

    mine = (block(lax.div(me, across), 8), lanes(lax.rem(me, across)))
    lax.fori_loop(1, n, hand_in, 0)
    tails_got[block(me, 8), :] = tails[mine]
    tails_wait(a2a_recv.at[6])
    tails_sum[mine] = jnp.sum(tails_got[...].reshape(n, 8, 128), axis=0)
    lax.fori_loop(1, n, hand_out, 0)

    landed(halo_kv)
    returned(1, out_k)
    returned(2, out_v)
    arrive(GRAD_FILTER)
    out_filter[...] = to_tokens(GRAD_FILTER).astype(BF16)

    tails_wait(a2a_recv.at[7])
    for i in range(3):
        out_short[i] = tails_sum[8 * i : 8 * i + 3, :]
    out_skip[...] = tails_sum[24:25, :]
    landed(final_copies)
    for copy in pending:
        copy.wait_send()
    for k in range(6):
        left(k)
    tails_wait(a2a_send.at[6])
    tails_wait(a2a_send.at[7])


def local(*args):
    n, tp = lax.axis_size("ctx"), lax.axis_size("tp")
    nz, ny = n // 4, tp // 2
    query, key, value, tap_q, tap_k, tap_v, filt, skip, weight, cot = args
    seq, ch = query.shape
    consts = [jnp.asarray(t) for t in tables(n, seq)]
    outer, outer_back, inner, twiddle = consts
    q_rows = GROUP * (n + 1)
    d_cols = nz * 128
    tokens4 = 4 * seq

    def vmem(shape, dtype=F32):
        return pltpu.VMEM(shape, dtype)

    scratch = [
        vmem(outer.shape, BF16), vmem(outer_back.shape, BF16), vmem(inner.shape, BF16),
        vmem(twiddle.shape),
        vmem((3, 16, ch), BF16), vmem((3, seq + 8, ch)), vmem((3, seq, ch)),
        vmem((seq, ch)), vmem((seq, ch)), vmem((seq, ch)), vmem((seq, ch)),
        vmem((3, seq + 8, ch)),
        vmem((6, 16 * n, 2 * seq), BF16), vmem((6, 16 * n, 2 * seq), BF16),
        vmem((ch, d_cols), BF16), vmem((tokens4, d_cols), BF16),
        vmem((tokens4, max(ch, d_cols))), vmem((tokens4, ch), BF16),
        vmem((2, seq, ch), BF16), vmem((seq, ch), BF16), vmem((seq, ch), BF16),
        vmem((tokens4, ch), BF16),
        vmem((tokens4, d_cols), BF16), vmem((max(ny - 1, 1), tokens4, 256), BF16),
        vmem((tokens4, 128)), vmem((tokens4, 128)), vmem((tokens4, 128), BF16),
        vmem((2, q_rows, 2 * seq)), vmem((2, q_rows, 2 * seq)), vmem((2, q_rows, 2 * seq)),
        vmem((2 * n * GROUP, 2 * seq)),
        vmem((32, ch)), vmem((8 * n, 128)), vmem((32, ch)),
        pltpu.SemaphoreType.DMA((4,)),
        pltpu.SemaphoreType.DMA((8,)), pltpu.SemaphoreType.DMA((8,)),
        pltpu.SemaphoreType.DMA((48,)), pltpu.SemaphoreType.DMA((48,)),
    ]
    shape = jax.ShapeDtypeStruct
    inside = pl.BlockSpec(memory_space=pltpu.VMEM)
    outside = pl.BlockSpec(memory_space=pl.ANY)
    out_shape = (
        shape(cot.shape, BF16),
        shape((seq, ch), BF16), shape((seq, ch), BF16), shape((seq, ch), BF16),
        shape((seq, ch), BF16),
        shape((1, ch), F32), shape((3, 3, ch), F32),
    )
    results = pl.pallas_call(
        lambda *refs: body(n, nz, ny, refs),
        out_shape=out_shape,
        in_specs=[inside] * 10 + [outside] * 4,
        out_specs=[inside] * 7,
        scratch_shapes=scratch,
        compiler_params=pltpu.CompilerParams(
            collective_id=0, has_side_effects=True, vmem_limit_bytes=60 * 1024 * 1024
        ),
        name="hyena",
    )(query, key, value, tap_q, tap_k, tap_v, filt, skip.reshape(1, ch), weight, cot, *consts)
    return results[:5] + (results[5].reshape(ch), results[6])


def solution(mesh):
    in_specs = (
        P("ctx", "tp"),
        P("ctx", "tp"),
        P("ctx", "tp"),
        P(None, "tp"),
        P(None, "tp"),
        P(None, "tp"),
        P("ctx", "tp"),
        P("tp"),
        P("tp", "ctx"),
        P("ctx", "tp"),
    )
    out_specs = (
        P("ctx", "tp"),
        P("ctx", "tp"),
        P("ctx", "tp"),
        P("ctx", "tp"),
        P("ctx", "tp"),
        P("tp"),
        P(None, None, "tp"),
    )
    return jax.shard_map(local, mesh=mesh, in_specs=in_specs, out_specs=out_specs, check_vma=False)
```

```python
import jax
import jax.numpy as jnp
import ml_dtypes
import numpy as np
from jax import lax
from jax.experimental import pallas as pl
from jax.experimental.pallas import tpu as pltpu
from jax.sharding import PartitionSpec as P

F32 = jnp.float32
BF16 = jnp.bfloat16
GROUP = 16
FILTER, GATED, MIXING, GRAD_MIX, GRAD_GATED, GRAD_FILTER = range(6)


def halves(matrix):
    high = matrix.astype(np.float32).astype(ml_dtypes.bfloat16)
    low = (matrix - high.astype(np.float64)).astype(np.float32).astype(ml_dtypes.bfloat16)
    return np.stack([high, low])


def tables(n, seq):
    total = 2 * n * seq
    q = np.arange(n + 1)
    m = np.arange(n)
    theta = 2 * np.pi * ((q[:, None] * m[None, :]) % (2 * n)) / (2 * n)
    forward = np.concatenate([np.cos(theta), -np.sin(theta)[1:n]])
    weight = np.where((q == 0) | (q == n), 1.0, 2.0)[:, None] / total
    back = np.concatenate([weight * np.cos(theta), (-weight * np.sin(theta))[1:n]]).T
    eye = np.eye(GROUP)
    j = np.arange(seq)
    phi = 2 * np.pi * ((j[:, None] * j[None, :]) % seq) / seq
    c, s = np.cos(phi), np.sin(phi)
    inner = np.block([[c, -s], [s, c]])
    inner_back = np.block([[c, s], [-s, c]])
    turn = 2 * np.pi * (q[:, None] * j[None, :]) / total
    twiddle = np.stack([np.cos(turn), np.sin(turn)]).astype(np.float32)
    twiddle = np.repeat(twiddle, GROUP, axis=1)
    return (
        halves(np.kron(forward, eye)),
        halves(np.kron(back, eye)),
        halves(np.stack([inner, inner_back])),
        twiddle,
    )


def split(value):
    high = value.astype(BF16)
    return high, (value - high.astype(F32)).astype(BF16)


def mm(left, right):
    return jnp.dot(left, right, preferred_element_type=F32)


def body(n, nz, ny, refs):
    (
        query_hbm, key_hbm, value_hbm, tap_q, tap_k, tap_v, filt_hbm, skip, weight, cot,
        outer_hbm, outer_back_hbm, inner_hbm, twiddle_hbm,
        mixed_hbm, grad_q_hbm, grad_k_hbm, grad_v_hbm, filter_hbm, skip_hbm, short_hbm,
        query, key, value, filt,
        mixed_out, out_grads, out_filter, out_skip, out_short,
        outer, outer_back, inner, twiddle,
        halo, ext, short, gated, mixing, grad_hidden, grad_mix, gext,
        sent, got, wide, cots, part, part_b, core_got, chip_sent, chip_got, hid,
        rows_b, rows_got, pair_sent, pair_got, final_b,
        spec_u, spec_h, spec_d, stage, tails, tails_got, tails_sum,
        const_sem, in_sem, out_sem, a2a_send, a2a_recv, send, recv,
    ) = refs
    seq, ch = query.shape
    half = ch // 2
    rows = 16 * n
    q_rows = GROUP * (n + 1)
    me = lax.axis_index("ctx")
    tp = lax.axis_index("tp")
    z, b = lax.div(me, 4), lax.rem(me, 4)
    xh, core = lax.div(b, 2), lax.rem(b, 2)
    y, xl = lax.div(tp, 2), lax.rem(tp, 2)
    counter = [0]
    pending = []

    def remote(src, dst, ctx, t):
        k = counter[0]
        counter[0] += 1
        copy = pltpu.make_async_remote_copy(
            src_ref=src, dst_ref=dst, send_sem=send.at[k], recv_sem=recv.at[k],
            device_id=(ctx, t), device_id_type=pl.DeviceIdType.MESH,
        )
        copy.start()
        pending.append(copy)
        return copy

    def at16(index):
        return pl.ds(pl.multiple_of(index * 16, 16), 16)

    def lanes(index, size=128):
        return pl.ds(pl.multiple_of(index * size, 128), size)

    def block(index, size=None):
        size = seq if size is None else size
        return pl.ds(pl.multiple_of(index * size, size), size)

    def spread(k, g=None):
        cols = pl.ds(0, 2 * seq) if g is None else pl.ds(g * seq, seq)
        sem = k if g is None else 8 + g

        def step(r, carry):
            dst = lax.rem(me + r, n)
            pltpu.make_async_remote_copy(
                src_ref=sent.at[k, at16(dst), cols], dst_ref=got.at[k, at16(me), cols],
                send_sem=a2a_send.at[sem], recv_sem=a2a_recv.at[sem],
                device_id=(dst, tp), device_id_type=pl.DeviceIdType.MESH,
            ).start()
            return carry

        lax.fori_loop(1, n, step, 0)
        got[k, at16(me), cols] = sent[k, at16(me), cols]

    def arrive(k, g=None):
        cols = pl.ds(0, 2 * seq) if g is None else pl.ds(g * seq, seq)
        whole = got.at[k, pl.ds(0, rows - 16), cols]
        pltpu.make_async_copy(whole, whole, a2a_recv.at[k if g is None else 8 + g]).wait()

    def left(k, g=None):
        cols = pl.ds(0, 2 * seq) if g is None else pl.ds(g * seq, seq)
        whole = sent.at[k, pl.ds(0, rows - 16), cols]
        pltpu.make_async_copy(whole, whole, a2a_send.at[k if g is None else 8 + g]).wait()

    def half_to_channels(x, k, g):
        sent[k, :, g * seq : (g + 1) * seq] = x.T.astype(BF16)

    def to_channels(x, k):
        for g in range(2):
            half_to_channels(x[:, g * half : (g + 1) * half], k, g)

    def to_tokens(k):
        return jnp.concatenate(
            [got[k, :, g * seq : (g + 1) * seq].astype(F32).T for g in range(2)], axis=1
        )

    def forward(k, spec):
        u = got[k]
        stage[...] = mm(outer[0], u) + mm(outer[1], u)
        cos, sin = twiddle[0], twiddle[1]
        zero = jnp.zeros((GROUP, seq), F32)
        for g in range(2):
            cols = pl.ds(g * seq, seq)
            real = stage[:q_rows, cols]
            imag = jnp.concatenate([zero, stage[q_rows:, cols], zero])
            pair = jnp.concatenate([real * cos + imag * sin, imag * cos - real * sin], axis=1)
            high, low = split(pair)
            spec[g] = mm(high, inner[0, 0]) + mm(low, inner[0, 0]) + mm(high, inner[1, 0])

    def product(first, second, g, conj):
        ar, ai = first[g, :, :seq], first[g, :, seq:]
        br, bi = second[g, :, :seq], second[g, :, seq:]
        if conj:
            return jnp.concatenate([ar * br + ai * bi, ar * bi - ai * br], axis=1)
        return jnp.concatenate([ar * br - ai * bi, ar * bi + ai * br], axis=1)

    def inverse(first, second, conj, k):
        cos, sin = twiddle[0], twiddle[1]
        for g in range(2):
            high, low = split(product(first, second, g, conj))
            turned = mm(high, inner[0, 1]) + mm(low, inner[0, 1]) + mm(high, inner[1, 1])
            real, imag = turned[:, :seq], turned[:, seq:]
            cols = pl.ds(g * seq, seq)
            stage[:q_rows, cols] = real * cos - imag * sin
            stage[q_rows:, cols] = (imag * cos + real * sin)[GROUP : q_rows - GROUP]
        high, low = split(stage[...])
        result = mm(outer_back[0], high) + mm(outer_back[0], low) + mm(outer_back[1], high)
        sent[k] = result.astype(BF16)

    barrier = pltpu.get_barrier_semaphore()

    def greet(r, carry):
        pl.semaphore_signal(
            barrier, inc=1, device_id=(lax.rem(me + r, n), tp),
            device_id_type=pl.DeviceIdType.MESH,
        )
        return carry

    lax.fori_loop(1, n, greet, 0)
    others = [(y, 1 - xl)] + [(lax.rem(y + r, ny), xl) for r in range(1, ny)]
    for oy, ox in others:
        pl.semaphore_signal(
            barrier, inc=1, device_id=(me, oy * 2 + ox), device_id_type=pl.DeviceIdType.MESH
        )
    loads = [
        pltpu.make_async_copy(src, dst, in_sem.at[i])
        for i, (src, dst) in enumerate(
            [
                (filt_hbm, filt), (weight, wide.at[:, lanes(z)]),
                (cot.at[:, lanes(b)], cots.at[block(b), lanes(tp)]),
                (query_hbm, query), (key_hbm, key), (value_hbm, value),
            ]
        )
    ]
    for copy in loads:
        copy.start()
    consts = [
        pltpu.make_async_copy(src, dst, const_sem.at[i])
        for i, (src, dst) in enumerate(
            [(outer_hbm, outer), (inner_hbm, inner), (twiddle_hbm, twiddle), (outer_back_hbm, outer_back)]
        )
    ]
    for copy in consts:
        copy.start()
    tails[...] = jnp.zeros_like(tails)
    loads[0].wait()
    to_channels(filt[...], FILTER)
    pl.semaphore_wait(barrier, n - 1 + len(others))

    following, preceding = lax.rem(me + 1, n), lax.rem(me + n - 1, n)
    halos = [
        remote(x.at[pl.ds(seq - 16, 16)], halo.at[i], following, tp)
        for i, x in enumerate((query_hbm, key_hbm, value_hbm))
    ]

    full = nz // 2 - 1
    up, down = lax.rem(z + 1, nz) * 4 + b, lax.rem(z + nz - 1, nz) * 4 + b

    def ring(s, c):
        piece = pl.ds(c * half, half)
        slot_up, slot_down = lanes(lax.rem(z + nz - s, nz)), lanes(lax.rem(z + s, nz))
        copies = []
        if s < full or c == 0:
            src = weight.at[piece] if s == 0 else wide.at[piece, slot_up]
            copies.append(remote(src, wide.at[piece, slot_up], up, tp))
        if s < full or c == 1:
            src = weight.at[piece] if s == 0 else wide.at[piece, slot_down]
            copies.append(remote(src, wide.at[piece, slot_down], down, tp))
        return copies

    def landed(copies):
        for copy in copies:
            copy.wait_recv()

    def mate(r):
        other = lax.rem(b + r, 4)
        return other, z * 4 + other

    hops = [ring(0, c) for c in range(2)]

    def advance(s):
        for c in range(2):
            landed(hops[c])
            hops[c] = ring(s, c) if s <= full else []

    cot_first = []
    for r in range(1, 4):
        other, ctx = mate(r)
        cot_first.append(remote(cot.at[:, lanes(other)], cots.at[block(b), lanes(tp)], ctx, tp))
    spread(FILTER)

    for copy in loads[1:]:
        copy.wait()
    landed(halos)
    taps = (tap_q, tap_k, tap_v)
    for i, x in enumerate((query, key, value)):
        ext[i, :8] = jnp.where(me == 0, 0.0, halo[i, 8:16].astype(F32))
        ext[i, 8:] = x[...].astype(F32)
        short[i] = (
            taps[i][0:1] * ext[i, pl.ds(8, seq)]
            + taps[i][1:2] * ext[i, pl.ds(7, seq)]
            + taps[i][2:3] * ext[i, pl.ds(6, seq)]
        )
    gated[...] = short[1] * short[2]
    to_channels(gated[...], GATED)

    landed(cot_first)
    cot_pair = remote(cots.at[:, lanes(tp)], cots.at[:, lanes(tp)], me, y * 2 + 1 - xl)
    for s in range(1, full):
        advance(s)
        if s == 1:
            cot_pair.wait_recv()
            cot_last = [
                remote(cots.at[:, lanes(y, 256)], cots.at[:, lanes(y, 256)], me, oy * 2 + ox)
                for oy, ox in others[1:]
            ]
    if full < 2:
        cot_pair.wait_recv()
        cot_last = [
            remote(cots.at[:, lanes(y, 256)], cots.at[:, lanes(y, 256)], me, oy * 2 + ox)
            for oy, ox in others[1:]
        ]

    for copy in consts:
        copy.wait()
    arrive(FILTER)
    forward(FILTER, spec_h)
    if full > 0:
        advance(full)
    spread(GATED)

    advance(full + 1)
    landed(cot_last)
    sibling = z * 4 + xh * 2 + 1 - core
    twin = z * 4 + (1 - xh) * 2 + core
    far = (1 - xh) * 2 + core
    core_copies = []
    for g in range(2):
        cols = pl.ds(g * half, half)
        for lo in range(g * half, (g + 1) * half, 256) if half >= 256 else [g * half]:
            some = pl.ds(lo, min(256, half))
            part[:, some] = lax.dot_general(
                cots[...], wide[some, :], (((1,), (1,)), ((), ())), preferred_element_type=F32
            )
        for i in range(2):
            theirs = block(i * 2 + 1 - core)
            part_b[theirs, cols] = part[theirs, cols].astype(BF16)
        core_copies.append(
            [remote(part_b.at[block(i * 2 + 1 - core), cols], core_got.at[g, i], sibling, tp) for i in range(2)]
        )
    chip_copies = []
    for g in range(2):
        cols = pl.ds(g * half, half)
        landed(core_copies[g])
        chip_sent[g] = (part[block(far), cols] + core_got[g, 1 - xh].astype(F32)).astype(BF16)
        chip_copies.append(remote(chip_sent.at[g], chip_got.at[g], twin, tp))

    arrive(GATED)
    forward(GATED, spec_u)
    inverse(spec_h, spec_u, False, MIXING)
    spread(MIXING)

    for g in range(2):
        cols = pl.ds(g * half, half)
        chip_copies[g].wait_recv()
        whole = part[block(b), cols] + core_got[g, xh].astype(F32) + chip_got[g].astype(F32)
        grad_hidden[:, cols] = whole
        whole = whole * short[0, :, cols]
        grad_mix[:, cols] = whole
        half_to_channels(whole, GRAD_MIX, g)
        spread(GRAD_MIX, g)
    tails[24, :] = jnp.sum(grad_mix[...] * gated[...], axis=0)

    arrive(MIXING)
    mixing[...] = to_tokens(MIXING) + skip[...] * gated[...]
    hid[block(b), :] = (short[0] * mixing[...]).astype(BF16)
    hid_sib = remote(hid.at[block(b)], hid.at[block(b)], sibling, tp)
    hid_twin = remote(hid.at[block(b)], hid.at[block(b)], twin, tp)
    gext[0, :seq] = grad_hidden[...] * mixing[...]
    halo_q = remote(gext.at[0, pl.ds(0, 8)], gext.at[0, pl.ds(seq, 8)], preceding, tp)

    def project(h):
        pair = block(h, 2 * seq)
        copies = []
        for r in list(range(1, ny)) + [0]:
            oy = lax.rem(y + r, ny)
            piece = mm(hid[pair, :], wide[:, lanes(oy, 256)])
            if r == 0:
                part[pair, lanes(oy, 256)] = piece
            else:
                rows_b[pair, lanes(oy, 256)] = piece.astype(BF16)
                copies.append(
                    remote(rows_b.at[pair, lanes(oy, 256)], rows_got.at[r - 1, pair], me, oy * 2 + xl)
                )
        return copies

    hid_sib.wait_recv()
    rows_near = project(xh)

    for g in range(2):
        arrive(GRAD_MIX, g)
    forward(GRAD_MIX, spec_d)
    inverse(spec_h, spec_d, True, GRAD_GATED)
    spread(GRAD_GATED)

    hid_twin.wait_recv()
    hid_far = remote(hid.at[block(far)], hid.at[block(far)], sibling, tp)

    def tap_sums(i):
        grads = gext[i, :seq]
        for o in range(3):
            tails[8 * i + o, :] = jnp.sum(grads * ext[i, pl.ds(8 - o, seq)], axis=0)

    tap_sums(0)
    hid_far.wait_recv()
    rows_far = project(1 - xh)
    inverse(spec_u, spec_d, True, GRAD_FILTER)
    spread(GRAD_FILTER)

    def collect(h, copies):
        pair = block(h, 2 * seq)
        landed(copies)
        for r in range(ny - 1):
            part[pair, lanes(y, 256)] += rows_got[r, pair].astype(F32)
        pair_sent[pair] = part[pair, lanes(y * 2 + 1 - xl)].astype(BF16)
        return remote(pair_sent.at[pair], pair_got.at[pair], me, y * 2 + 1 - xl)

    def finish(h, copy):
        pair = block(h, 2 * seq)
        copy.wait_recv()
        final_b[pair] = (part[pair, lanes(tp)] + pair_got[pair].astype(F32)).astype(BF16)

    def hand(other):
        return remote(final_b.at[block(other)], mixed_out.at[:, lanes(b)], z * 4 + other, tp)

    pair_near = collect(xh, rows_near)

    out_copies = []

    def store(src, dst):
        copy = pltpu.make_async_copy(src, dst, out_sem.at[len(out_copies)])
        copy.start()
        out_copies.append(copy)

    def returned(i, hbm):
        gext[i, seq:] = jnp.where(me == n - 1, 0.0, gext[i, seq:])
        out_grads[i] = (
            taps[i][0:1] * gext[i, pl.ds(0, seq)]
            + taps[i][1:2] * gext[i, pl.ds(1, seq)]
            + taps[i][2:3] * gext[i, pl.ds(2, seq)]
        ).astype(BF16)
        store(out_grads.at[i], hbm)

    halo_q.wait_recv()
    returned(0, grad_q_hbm)

    arrive(GRAD_GATED)
    grad = to_tokens(GRAD_GATED) + skip[...] * grad_mix[...]
    gext[1, :seq] = grad * short[2]
    gext[2, :seq] = grad * short[1]
    halo_kv = [
        remote(gext.at[i, pl.ds(0, 8)], gext.at[i, pl.ds(seq, 8)], preceding, tp) for i in (1, 2)
    ]
    tap_sums(1)
    tap_sums(2)

    across = ch // 128

    def tile(ref, d):
        return ref.at[block(lax.div(d, across), 8), lanes(lax.rem(d, across))]

    def hand_in(r, carry):
        dst = lax.rem(me + r, n)
        pltpu.make_async_remote_copy(
            src_ref=tile(tails, dst), dst_ref=tails_got.at[block(me, 8)],
            send_sem=a2a_send.at[6], recv_sem=a2a_recv.at[6],
            device_id=(dst, tp), device_id_type=pl.DeviceIdType.MESH,
        ).start()
        return carry

    def hand_out(r, carry):
        dst = lax.rem(me + r, n)
        pltpu.make_async_remote_copy(
            src_ref=tile(tails_sum, me), dst_ref=tile(tails_sum, me),
            send_sem=a2a_send.at[7], recv_sem=a2a_recv.at[7],
            device_id=(dst, tp), device_id_type=pl.DeviceIdType.MESH,
        ).start()
        return carry

    def tails_wait(sem):
        whole = tails_got.at[pl.ds(0, 8 * (n - 1))]
        pltpu.make_async_copy(whole, whole, sem).wait()

    mine = (block(lax.div(me, across), 8), lanes(lax.rem(me, across)))
    lax.fori_loop(1, n, hand_in, 0)
    tails_got[block(me, 8), :] = tails[mine]

    pair_far = collect(1 - xh, rows_far)
    finish(xh, pair_near)
    mixed_out[:, lanes(b)] = final_b[block(b), :]
    final_copies = [hand(xh * 2 + 1 - core)]

    tails_wait(a2a_recv.at[6])
    tails_sum[mine] = jnp.sum(tails_got[...].reshape(n, 8, 128), axis=0)
    lax.fori_loop(1, n, hand_out, 0)

    landed(halo_kv)
    returned(1, grad_k_hbm)
    returned(2, grad_v_hbm)
    finish(1 - xh, pair_far)
    final_copies += [hand(far), hand((1 - xh) * 2 + 1 - core)]
    arrive(GRAD_FILTER)
    out_filter[...] = to_tokens(GRAD_FILTER).astype(BF16)
    store(out_filter, filter_hbm)

    tails_wait(a2a_recv.at[7])
    for i in range(3):
        out_short[i] = tails_sum[8 * i : 8 * i + 3, :]
    out_skip[...] = tails_sum[24:25, :]
    store(out_short, short_hbm)
    store(out_skip, skip_hbm)
    landed(final_copies)
    store(mixed_out, mixed_hbm)
    for copy in pending:
        copy.wait_send()
    for k in (FILTER, GATED, MIXING, GRAD_GATED, GRAD_FILTER):
        left(k)
    for g in range(2):
        left(GRAD_MIX, g)
    tails_wait(a2a_send.at[6])
    tails_wait(a2a_send.at[7])
    for copy in out_copies:
        copy.wait()


def handover(*refs):
    count = 7
    sources, targets, held = refs[:count], refs[count : 2 * count], refs[2 * count : 3 * count]
    in_sem, out_sem = refs[3 * count :]
    copies = [pltpu.make_async_copy(sources[i], held[i], in_sem.at[i]) for i in range(count)]
    for copy in copies:
        copy.start()
    outs = []
    for i in range(count):
        copies[i].wait()
        outs.append(pltpu.make_async_copy(held[i], targets[i], out_sem.at[i]))
        outs[-1].start()
    for copy in outs:
        copy.wait()


def local(*args):
    n, tp = lax.axis_size("ctx"), lax.axis_size("tp")
    nz, ny = n // 4, tp // 2
    query, key, value, tap_q, tap_k, tap_v, filt, skip, weight, cot = args
    seq, ch = query.shape
    consts = [jnp.asarray(t) for t in tables(n, seq)]
    outer, outer_back, inner, twiddle = consts
    q_rows = GROUP * (n + 1)
    d_cols = nz * 128
    tokens4 = 4 * seq
    half = ch // 2

    def vmem(shape, dtype=F32):
        return pltpu.VMEM(shape, dtype)

    scratch = [
        vmem((seq, ch), BF16), vmem((seq, ch), BF16), vmem((seq, ch), BF16), vmem((seq, ch)),
        vmem(cot.shape, BF16), vmem((3, seq, ch), BF16), vmem((seq, ch), BF16),
        vmem((1, ch)), vmem((3, 3, ch)),
        vmem(outer.shape, BF16), vmem(outer_back.shape, BF16), vmem(inner.shape, BF16),
        vmem(twiddle.shape),
        vmem((3, 16, ch), BF16), vmem((3, seq + 8, ch)), vmem((3, seq, ch)),
        vmem((seq, ch)), vmem((seq, ch)), vmem((seq, ch)), vmem((seq, ch)),
        vmem((3, seq + 8, ch)),
        vmem((6, 16 * n, 2 * seq), BF16), vmem((6, 16 * n, 2 * seq), BF16),
        vmem((ch, d_cols), BF16), vmem((tokens4, d_cols), BF16),
        vmem((tokens4, max(ch, d_cols))), vmem((tokens4, ch), BF16),
        vmem((2, 2, seq, half), BF16), vmem((2, seq, half), BF16), vmem((2, seq, half), BF16),
        vmem((tokens4, ch), BF16),
        vmem((tokens4, d_cols), BF16), vmem((max(ny - 1, 1), tokens4, 256), BF16),
        vmem((tokens4, 128), BF16), vmem((tokens4, 128), BF16), vmem((tokens4, 128), BF16),
        vmem((2, q_rows, 2 * seq)), vmem((2, q_rows, 2 * seq)), vmem((2, q_rows, 2 * seq)),
        vmem((2 * n * GROUP, 2 * seq)),
        vmem((32, ch)), vmem((8 * n, 128)), vmem((32, ch)),
        pltpu.SemaphoreType.DMA((4,)), pltpu.SemaphoreType.DMA((6,)), pltpu.SemaphoreType.DMA((7,)),
        pltpu.SemaphoreType.DMA((10,)), pltpu.SemaphoreType.DMA((10,)),
        pltpu.SemaphoreType.DMA((64,)), pltpu.SemaphoreType.DMA((64,)),
    ]
    shape = jax.ShapeDtypeStruct
    inside = pl.BlockSpec(memory_space=pltpu.VMEM)
    outside = pl.BlockSpec(memory_space=pl.ANY)
    out_shape = (
        shape(cot.shape, BF16),
        shape((seq, ch), BF16), shape((seq, ch), BF16), shape((seq, ch), BF16),
        shape((seq, ch), BF16),
        shape((1, ch), F32), shape((3, 3, ch), F32),
    )
    results = pl.pallas_call(
        lambda *refs: body(n, nz, ny, refs),
        out_shape=out_shape,
        in_specs=[outside] * 3 + [inside] * 3 + [outside, inside, outside, outside] + [outside] * 4,
        out_specs=[outside] * 7,
        scratch_shapes=scratch,
        compiler_params=pltpu.CompilerParams(
            collective_id=0, has_side_effects=True, vmem_limit_bytes=60 * 1024 * 1024
        ),
        name="hyena",
    )(query, key, value, tap_q, tap_k, tap_v, filt, skip.reshape(1, ch), weight, cot, *consts)
    results = pl.pallas_call(
        handover,
        out_shape=out_shape,
        in_specs=[outside] * 7,
        out_specs=[outside] * 7,
        scratch_shapes=[vmem(o.shape, o.dtype) for o in out_shape]
        + [pltpu.SemaphoreType.DMA((7,)), pltpu.SemaphoreType.DMA((7,))],
        name="handover",
    )(*results)
    return results[:5] + (results[5].reshape(ch), results[6])


def solution(mesh):
    in_specs = (
        P("ctx", "tp"),
        P("ctx", "tp"),
        P("ctx", "tp"),
        P(None, "tp"),
        P(None, "tp"),
        P(None, "tp"),
        P("ctx", "tp"),
        P("tp"),
        P("tp", "ctx"),
        P("ctx", "tp"),
    )
    out_specs = (
        P("ctx", "tp"),
        P("ctx", "tp"),
        P("ctx", "tp"),
        P("ctx", "tp"),
        P("ctx", "tp"),
        P("tp"),
        P(None, None, "tp"),
    )
    return jax.shard_map(local, mesh=mesh, in_specs=in_specs, out_specs=out_specs, check_vma=False)
```

```python
import jax
import jax.numpy as jnp
import ml_dtypes
import numpy as np
from jax import lax
from jax.experimental import pallas as pl
from jax.experimental.pallas import tpu as pltpu
from jax.sharding import PartitionSpec as P

F32 = jnp.float32
BF16 = jnp.bfloat16
GROUP = 16
FILTER, GATED, MIXING, GRAD_MIX, GRAD_GATED, GRAD_FILTER = range(6)
FILTER_PLACE, GATED_PLACE, ORDER, LATE_FILTER = 0, 4, 2, False


def halves(matrix):
    high = matrix.astype(np.float32).astype(ml_dtypes.bfloat16)
    low = (matrix - high.astype(np.float64)).astype(np.float32).astype(ml_dtypes.bfloat16)
    return np.stack([high, low])


def tables(n, seq):
    total = 2 * n * seq
    q = np.arange(n + 1)
    m = np.arange(n)
    theta = 2 * np.pi * ((q[:, None] * m[None, :]) % (2 * n)) / (2 * n)
    forward = np.concatenate([np.cos(theta), -np.sin(theta)[1:n]])
    weight = np.where((q == 0) | (q == n), 1.0, 2.0)[:, None] / total
    back = np.concatenate([weight * np.cos(theta), (-weight * np.sin(theta))[1:n]]).T
    eye = np.eye(GROUP)
    j = np.arange(seq)
    phi = 2 * np.pi * ((j[:, None] * j[None, :]) % seq) / seq
    c, s = np.cos(phi), np.sin(phi)
    inner = np.block([[c, -s], [s, c]])
    inner_back = np.block([[c, s], [-s, c]])
    turn = 2 * np.pi * (q[:, None] * j[None, :]) / total
    twiddle = np.stack([np.cos(turn), np.sin(turn)]).astype(np.float32)
    twiddle = np.repeat(twiddle, GROUP, axis=1)
    return (
        halves(np.kron(forward, eye)),
        halves(np.kron(back, eye)),
        halves(np.stack([inner, inner_back])),
        twiddle,
    )


def split(value):
    high = value.astype(BF16)
    return high, (value - high.astype(F32)).astype(BF16)


def mm(left, right):
    return jnp.dot(left, right, preferred_element_type=F32)


def body(n, nz, ny, refs):
    (
        query_hbm, key_hbm, value_hbm, tap_q, tap_k, tap_v, filt_hbm, skip, weight, cot,
        outer_hbm, outer_back_hbm, inner_hbm, twiddle_hbm,
        mixed_hbm, grad_q_hbm, grad_k_hbm, grad_v_hbm, filter_hbm, skip_hbm, short_hbm,
        query, key, value, filt,
        mixed_out, out_grads, out_filter, out_skip, out_short,
        outer, outer_back, inner, twiddle,
        halo, ext, short, gated, mixing, grad_hidden, grad_mix, gext,
        sent, got, wide, cots, part, part_b, core_got, chip_sent, chip_got, hid,
        rows_b, rows_got, pair_sent, pair_got, final_b,
        spec_u, spec_h, spec_d, stage, tails, tails_got, tails_sum,
        const_sem, in_sem, out_sem, a2a_send, a2a_recv, send, recv,
    ) = refs
    seq, ch = query.shape
    half = ch // 2
    rows = 16 * n
    q_rows = GROUP * (n + 1)
    me = lax.axis_index("ctx")
    tp = lax.axis_index("tp")
    z, b = lax.div(me, 4), lax.rem(me, 4)
    xh, core = lax.div(b, 2), lax.rem(b, 2)
    y, xl = lax.div(tp, 2), lax.rem(tp, 2)
    counter = [0]
    pending = []

    def remote(src, dst, ctx, t):
        k = counter[0]
        counter[0] += 1
        copy = pltpu.make_async_remote_copy(
            src_ref=src, dst_ref=dst, send_sem=send.at[k], recv_sem=recv.at[k],
            device_id=(ctx, t), device_id_type=pl.DeviceIdType.MESH,
        )
        copy.start()
        pending.append(copy)
        return copy

    def at16(index):
        return pl.ds(pl.multiple_of(index * 16, 16), 16)

    def lanes(index, size=128):
        return pl.ds(pl.multiple_of(index * size, 128), size)

    def block(index, size=None):
        size = seq if size is None else size
        return pl.ds(pl.multiple_of(index * size, size), size)

    def peer(r):
        off = lax.div(r, 2)
        return lax.rem(me + n // 2 + off * (1 - 2 * lax.rem(r, 2)) + n, n)

    def spread(k, g=None):
        cols = pl.ds(0, 2 * seq) if g is None else pl.ds(g * seq, seq)
        sem = k if g is None else 8 + g

        def step(r, carry):
            dst = peer(r)
            pltpu.make_async_remote_copy(
                src_ref=sent.at[k, at16(dst), cols], dst_ref=got.at[k, at16(me), cols],
                send_sem=a2a_send.at[sem], recv_sem=a2a_recv.at[sem],
                device_id=(dst, tp), device_id_type=pl.DeviceIdType.MESH,
            ).start()
            return carry

        lax.fori_loop(1, n, step, 0)
        got[k, at16(me), cols] = sent[k, at16(me), cols]

    def arrive(k, g=None):
        cols = pl.ds(0, 2 * seq) if g is None else pl.ds(g * seq, seq)
        whole = got.at[k, pl.ds(0, rows - 16), cols]
        pltpu.make_async_copy(whole, whole, a2a_recv.at[k if g is None else 8 + g]).wait()

    def left(k, g=None):
        cols = pl.ds(0, 2 * seq) if g is None else pl.ds(g * seq, seq)
        whole = sent.at[k, pl.ds(0, rows - 16), cols]
        pltpu.make_async_copy(whole, whole, a2a_send.at[k if g is None else 8 + g]).wait()

    def half_to_channels(x, k, g):
        sent[k, :, g * seq : (g + 1) * seq] = x.T.astype(BF16)

    def to_channels(x, k):
        for g in range(2):
            half_to_channels(x[:, g * half : (g + 1) * half], k, g)

    def to_tokens(k):
        return jnp.concatenate(
            [got[k, :, g * seq : (g + 1) * seq].astype(F32).T for g in range(2)], axis=1
        )

    def forward(k, spec):
        u = got[k]
        stage[...] = mm(outer[0], u) + mm(outer[1], u)
        cos, sin = twiddle[0], twiddle[1]
        zero = jnp.zeros((GROUP, seq), F32)
        for g in range(2):
            cols = pl.ds(g * seq, seq)
            real = stage[:q_rows, cols]
            imag = jnp.concatenate([zero, stage[q_rows:, cols], zero])
            pair = jnp.concatenate([real * cos + imag * sin, imag * cos - real * sin], axis=1)
            high, low = split(pair)
            spec[g] = mm(high, inner[0, 0]) + mm(low, inner[0, 0]) + mm(high, inner[1, 0])

    def product(first, second, g, conj):
        ar, ai = first[g, :, :seq], first[g, :, seq:]
        br, bi = second[g, :, :seq], second[g, :, seq:]
        if conj:
            return jnp.concatenate([ar * br + ai * bi, ar * bi - ai * br], axis=1)
        return jnp.concatenate([ar * br - ai * bi, ar * bi + ai * br], axis=1)

    def inverse(first, second, conj, k):
        cos, sin = twiddle[0], twiddle[1]
        for g in range(2):
            high, low = split(product(first, second, g, conj))
            turned = mm(high, inner[0, 1]) + mm(low, inner[0, 1]) + mm(high, inner[1, 1])
            real, imag = turned[:, :seq], turned[:, seq:]
            cols = pl.ds(g * seq, seq)
            stage[:q_rows, cols] = real * cos - imag * sin
            stage[q_rows:, cols] = (imag * cos + real * sin)[GROUP : q_rows - GROUP]
        high, low = split(stage[...])
        result = mm(outer_back[0], high) + mm(outer_back[0], low) + mm(outer_back[1], high)
        sent[k] = result.astype(BF16)

    barrier = pltpu.get_barrier_semaphore()

    def greet(r, carry):
        pl.semaphore_signal(
            barrier, inc=1, device_id=(lax.rem(me + r, n), tp),
            device_id_type=pl.DeviceIdType.MESH,
        )
        return carry

    lax.fori_loop(1, n, greet, 0)
    others = [(y, 1 - xl)] + [(lax.rem(y + r, ny), xl) for r in range(1, ny)]
    for oy, ox in others:
        pl.semaphore_signal(
            barrier, inc=1, device_id=(me, oy * 2 + ox), device_id_type=pl.DeviceIdType.MESH
        )
    loads = [
        pltpu.make_async_copy(src, dst, in_sem.at[i])
        for i, (src, dst) in enumerate(
            [
                (filt_hbm, filt), (weight, wide.at[:, lanes(z)]),
                (cot.at[:, lanes(b)], cots.at[block(b), lanes(tp)]),
                (query_hbm, query), (key_hbm, key), (value_hbm, value),
            ]
        )
    ]
    for copy in loads:
        copy.start()
    consts = [
        pltpu.make_async_copy(src, dst, const_sem.at[i])
        for i, (src, dst) in enumerate(
            [(outer_hbm, outer), (inner_hbm, inner), (twiddle_hbm, twiddle), (outer_back_hbm, outer_back)]
        )
    ]
    for copy in consts:
        copy.start()
    tails[...] = jnp.zeros_like(tails)
    loads[0].wait()
    to_channels(filt[...], FILTER)
    pl.semaphore_wait(barrier, n - 1 + len(others))

    following, preceding = lax.rem(me + 1, n), lax.rem(me + n - 1, n)
    halos = [
        remote(x.at[pl.ds(seq - 16, 16)], halo.at[i], following, tp)
        for i, x in enumerate((query_hbm, key_hbm, value_hbm))
    ]

    full = nz // 2 - 1
    up, down = lax.rem(z + 1, nz) * 4 + b, lax.rem(z + nz - 1, nz) * 4 + b

    def ring(s, c):
        piece = pl.ds(c * half, half)
        slot_up, slot_down = lanes(lax.rem(z + nz - s, nz)), lanes(lax.rem(z + s, nz))
        copies = []
        if s < full or c == 0:
            src = weight.at[piece] if s == 0 else wide.at[piece, slot_up]
            copies.append(remote(src, wide.at[piece, slot_up], up, tp))
        if s < full or c == 1:
            src = weight.at[piece] if s == 0 else wide.at[piece, slot_down]
            copies.append(remote(src, wide.at[piece, slot_down], down, tp))
        return copies

    def landed(copies):
        for copy in copies:
            copy.wait_recv()

    def mate(r):
        other = lax.rem(b + r, 4)
        return other, z * 4 + other

    hops = [ring(0, c) for c in range(2)]

    def advance(s):
        for c in range(2):
            landed(hops[c])
            hops[c] = ring(s, c) if s <= full else []

    def send_at(place):
        if place == FILTER_PLACE:
            spread(FILTER)
        if place == GATED_PLACE:
            spread(GATED)

    cot_first = []
    for r in range(1, 4):
        other, ctx = mate(r)
        cot_first.append(remote(cot.at[:, lanes(other)], cots.at[block(b), lanes(tp)], ctx, tp))
    send_at(0)

    for copy in loads[1:]:
        copy.wait()
    landed(halos)
    taps = (tap_q, tap_k, tap_v)
    for i, x in enumerate((query, key, value)):
        ext[i, :8] = jnp.where(me == 0, 0.0, halo[i, 8:16].astype(F32))
        ext[i, 8:] = x[...].astype(F32)
        short[i] = (
            taps[i][0:1] * ext[i, pl.ds(8, seq)]
            + taps[i][1:2] * ext[i, pl.ds(7, seq)]
            + taps[i][2:3] * ext[i, pl.ds(6, seq)]
        )
    gated[...] = short[1] * short[2]
    to_channels(gated[...], GATED)

    landed(cot_first)
    cot_pair = remote(cots.at[:, lanes(tp)], cots.at[:, lanes(tp)], me, y * 2 + 1 - xl)
    send_at(1)
    for s in range(1, full):
        advance(s)
        send_at(1 + s)
        if s == 1:
            cot_pair.wait_recv()
            cot_last = [
                remote(cots.at[:, lanes(y, 256)], cots.at[:, lanes(y, 256)], me, oy * 2 + ox)
                for oy, ox in others[1:]
            ]
    if full < 2:
        cot_pair.wait_recv()
        cot_last = [
            remote(cots.at[:, lanes(y, 256)], cots.at[:, lanes(y, 256)], me, oy * 2 + ox)
            for oy, ox in others[1:]
        ]

    def slots(offsets):
        places = [lax.rem(z + nz + o, nz) for o in offsets]
        return (
            jnp.concatenate([cots[:, lanes(p)] for p in places], axis=1),
            lambda some: jnp.concatenate([wide[some, lanes(p)] for p in places], axis=1),
        )

    def add_slots(offsets, first):
        tokens, features = slots(offsets)
        for lo in range(0, ch, 256):
            some = pl.ds(lo, 256)
            term = lax.dot_general(
                tokens, features(some), (((1,), (1,)), ((), ())), preferred_element_type=F32
            )
            part[:, some] = term if first else part[:, some] + term

    if full > 0:
        advance(full)
    send_at(4)
    landed(cot_last)
    add_slots([0] + [o * w for o in range(1, full + 1) for w in (1, -1)], True)
    for copy in consts:
        copy.wait()
    if FILTER_PLACE < 2:
        arrive(FILTER)
        forward(FILTER, spec_h)

    advance(full + 1)
    sibling = z * 4 + xh * 2 + 1 - core
    twin = z * 4 + (1 - xh) * 2 + core
    far = (1 - xh) * 2 + core
    core_copies = []
    tokens, features = slots([full + 1])
    for g in range(2):
        cols = pl.ds(g * half, half)
        term = lax.dot_general(
            tokens, features(cols), (((1,), (1,)), ((), ())), preferred_element_type=F32
        )
        part[:, cols] += term
        for i in range(2):
            theirs = block(i * 2 + 1 - core)
            part_b[theirs, cols] = part[theirs, cols].astype(BF16)
        core_copies.append(
            [remote(part_b.at[block(i * 2 + 1 - core), cols], core_got.at[g, i], sibling, tp) for i in range(2)]
        )
    send_at(5)
    chip_copies = []
    for g in range(2):
        cols = pl.ds(g * half, half)
        landed(core_copies[g])
        chip_sent[g] = (part[block(far), cols] + core_got[g, 1 - xh].astype(F32)).astype(BF16)
        chip_copies.append(remote(chip_sent.at[g], chip_got.at[g], twin, tp))

    def mix(first, second):
        if first:
            arrive(GATED)
            forward(GATED, spec_u)
        if second:
            inverse(spec_h, spec_u, False, MIXING)
            spread(MIXING)

    if FILTER_PLACE >= 2 and ORDER != 0:
        arrive(FILTER)
        forward(FILTER, spec_h)
    mix(ORDER != 0, ORDER == 2)

    for g in range(2):
        cols = pl.ds(g * half, half)
        chip_copies[g].wait_recv()
        whole = part[block(b), cols] + core_got[g, xh].astype(F32) + chip_got[g].astype(F32)
        grad_hidden[:, cols] = whole
        whole = whole * short[0, :, cols]
        grad_mix[:, cols] = whole
        half_to_channels(whole, GRAD_MIX, g)
        spread(GRAD_MIX, g)
    if FILTER_PLACE >= 2 and ORDER == 0:
        arrive(FILTER)
        forward(FILTER, spec_h)
    mix(ORDER == 0, ORDER != 2)
    tails[3, :] = jnp.sum(grad_mix[...] * gated[...], axis=0)

    def back():
        for g in range(2):
            arrive(GRAD_MIX, g)
        forward(GRAD_MIX, spec_d)
        inverse(spec_h, spec_d, True, GRAD_GATED)
        spread(GRAD_GATED)

    if ORDER != 2:
        back()

    arrive(MIXING)
    mixing[...] = to_tokens(MIXING) + skip[...] * gated[...]
    hid[block(b), :] = (short[0] * mixing[...]).astype(BF16)
    hid_sib = remote(hid.at[block(b)], hid.at[block(b)], sibling, tp)
    hid_twin = [
        remote(hid.at[block(b), pl.ds(g * half, half)], hid.at[block(b), pl.ds(g * half, half)], twin, tp)
        for g in range(2)
    ]
    gext[0, :seq] = grad_hidden[...] * mixing[...]
    halo_q = remote(gext.at[0, pl.ds(0, 8)], gext.at[0, pl.ds(seq, 8)], preceding, tp)

    def project(h):
        pair = block(h, 2 * seq)
        copies = []
        for r in list(range(1, ny)) + [0]:
            oy = lax.rem(y + r, ny)
            piece = mm(hid[pair, :], wide[:, lanes(oy, 256)])
            if r == 0:
                part[pair, lanes(oy, 256)] = piece
            else:
                rows_b[pair, lanes(oy, 256)] = piece.astype(BF16)
                copies.append(
                    remote(rows_b.at[pair, lanes(oy, 256)], rows_got.at[r - 1, pair], me, oy * 2 + xl)
                )
        return copies

    hid_sib.wait_recv()
    rows_near = project(xh)

    if ORDER == 2:
        back()

    hid_far = []
    for g in range(2):
        hid_twin[g].wait_recv()
        place = hid.at[block(far), pl.ds(g * half, half)]
        hid_far.append(remote(place, place, sibling, tp))

    def hand_in(g):
        def step(r, carry):
            to_z = lax.rem(z + r, nz)
            dst = to_z * 4 + 3 - 3 * g

            @pl.when(dst != me)
            def _():
                pltpu.make_async_remote_copy(
                    src_ref=tails.at[pl.ds(8 * g, 8), lanes(to_z)], dst_ref=tails_got.at[g, block(me, 8)],
                    send_sem=a2a_send.at[6 + g], recv_sem=a2a_recv.at[6 + g],
                    device_id=(dst, tp), device_id_type=pl.DeviceIdType.MESH,
                ).start()

            return carry

        lax.fori_loop(0, nz, step, 0)
        tails_got[g, block(me, 8), :] = tails[8 * g : 8 * g + 8, lanes(z)]

    def tails_wait(sem, count):
        whole = tails_got.at[0, pl.ds(0, 8 * count)]
        pltpu.make_async_copy(whole, whole, sem).wait()

    def owner_wait(g, sem, count, other):
        owner = b == 3 - 3 * g

        @pl.when(owner)
        def _():
            tails_wait(sem, count)

        if other:
            @pl.when(jnp.logical_not(owner))
            def _():
                tails_wait(sem, other)

    def hand_out(g):
        place = tails_sum.at[pl.ds(8 * g, 8), lanes(z)]

        @pl.when(b == 3 - 3 * g)
        def _():
            tails_wait(a2a_recv.at[6 + g], n - 1)
            tails_sum[8 * g : 8 * g + 8, lanes(z)] = jnp.sum(tails_got[g].reshape(n, 8, 128), axis=0)

            def step(r, carry):
                pltpu.make_async_remote_copy(
                    src_ref=place, dst_ref=place,
                    send_sem=a2a_send.at[10 + g], recv_sem=a2a_recv.at[10 + g],
                    device_id=(peer(r), tp), device_id_type=pl.DeviceIdType.MESH,
                ).start()
                return carry

            lax.fori_loop(1, n, step, 0)

    def tap_sums(i):
        grads = gext[i, :seq]
        for o in range(3):
            tails[(0, 8, 11)[i] + o, :] = jnp.sum(grads * ext[i, pl.ds(8 - o, seq)], axis=0)

    tap_sums(0)
    hand_in(0)
    landed(hid_far)
    rows_far = project(1 - xh)
    inverse(spec_u, spec_d, True, GRAD_FILTER)
    if not LATE_FILTER:
        spread(GRAD_FILTER)

    def collect(h, copies):
        pair = block(h, 2 * seq)
        landed(copies)
        for r in range(ny - 1):
            part[pair, lanes(y, 256)] += rows_got[r, pair].astype(F32)
        pair_sent[pair] = part[pair, lanes(y * 2 + 1 - xl)].astype(BF16)
        return remote(pair_sent.at[pair], pair_got.at[pair], me, y * 2 + 1 - xl)

    def finish(h, copy):
        pair = block(h, 2 * seq)
        copy.wait_recv()
        final_b[pair] = (part[pair, lanes(tp)] + pair_got[pair].astype(F32)).astype(BF16)

    def hand(other):
        return remote(final_b.at[block(other)], mixed_out.at[:, lanes(b)], z * 4 + other, tp)

    pair_near = collect(xh, rows_near)

    out_copies = []

    def store(src, dst):
        copy = pltpu.make_async_copy(src, dst, out_sem.at[len(out_copies)])
        copy.start()
        out_copies.append(copy)

    def returned(i, hbm):
        gext[i, seq:] = jnp.where(me == n - 1, 0.0, gext[i, seq:])
        out_grads[i] = (
            taps[i][0:1] * gext[i, pl.ds(0, seq)]
            + taps[i][1:2] * gext[i, pl.ds(1, seq)]
            + taps[i][2:3] * gext[i, pl.ds(2, seq)]
        ).astype(BF16)
        store(out_grads.at[i], hbm)

    halo_q.wait_recv()
    returned(0, grad_q_hbm)
    hand_out(0)

    arrive(GRAD_GATED)
    if LATE_FILTER:
        spread(GRAD_FILTER)
    grad = to_tokens(GRAD_GATED) + skip[...] * grad_mix[...]
    gext[1, :seq] = grad * short[2]
    gext[2, :seq] = grad * short[1]
    halo_kv = [
        remote(gext.at[i, pl.ds(0, 8)], gext.at[i, pl.ds(seq, 8)], preceding, tp) for i in (1, 2)
    ]
    tap_sums(1)
    tap_sums(2)

    hand_in(1)

    pair_far = collect(1 - xh, rows_far)
    finish(xh, pair_near)
    mixed_out[:, lanes(b)] = final_b[block(b), :]
    final_copies = [hand(xh * 2 + 1 - core)]

    hand_out(1)

    landed(halo_kv)
    returned(1, grad_k_hbm)
    returned(2, grad_v_hbm)
    finish(1 - xh, pair_far)
    final_copies += [hand(far), hand((1 - xh) * 2 + 1 - core)]
    arrive(GRAD_FILTER)
    out_filter[...] = to_tokens(GRAD_FILTER).astype(BF16)
    store(out_filter, filter_hbm)

    for g in range(2):
        owner_wait(g, a2a_recv.at[10 + g], nz - 1, nz)
    for i, row in enumerate((0, 8, 11)):
        out_short[i] = tails_sum[row : row + 3, :]
    out_skip[...] = tails_sum[3:4, :]
    store(out_short, short_hbm)
    store(out_skip, skip_hbm)
    landed(final_copies)
    store(mixed_out, mixed_hbm)
    for copy in pending:
        copy.wait_send()
    for k in (FILTER, GATED, MIXING, GRAD_GATED, GRAD_FILTER):
        left(k)
    for g in range(2):
        left(GRAD_MIX, g)
    for g in range(2):
        owner_wait(g, a2a_send.at[6 + g], nz - 1, nz)
        owner_wait(g, a2a_send.at[10 + g], n - 1, 0)
    for copy in out_copies:
        copy.wait()


def handover(*refs):
    count = 7
    sources, targets, held = refs[:count], refs[count : 2 * count], refs[2 * count : 3 * count]
    in_sem, out_sem = refs[3 * count :]
    copies = [pltpu.make_async_copy(sources[i], held[i], in_sem.at[i]) for i in range(count)]
    for copy in copies:
        copy.start()
    outs = []
    for i in range(count):
        copies[i].wait()
        outs.append(pltpu.make_async_copy(held[i], targets[i], out_sem.at[i]))
        outs[-1].start()
    for copy in outs:
        copy.wait()


def local(*args):
    n, tp = lax.axis_size("ctx"), lax.axis_size("tp")
    nz, ny = n // 4, tp // 2
    query, key, value, tap_q, tap_k, tap_v, filt, skip, weight, cot = args
    seq, ch = query.shape
    consts = [jnp.asarray(t) for t in tables(n, seq)]
    outer, outer_back, inner, twiddle = consts
    q_rows = GROUP * (n + 1)
    d_cols = nz * 128
    tokens4 = 4 * seq
    half = ch // 2

    def vmem(shape, dtype=F32):
        return pltpu.VMEM(shape, dtype)

    scratch = [
        vmem((seq, ch), BF16), vmem((seq, ch), BF16), vmem((seq, ch), BF16), vmem((seq, ch)),
        vmem(cot.shape, BF16), vmem((3, seq, ch), BF16), vmem((seq, ch), BF16),
        vmem((1, ch)), vmem((3, 3, ch)),
        vmem(outer.shape, BF16), vmem(outer_back.shape, BF16), vmem(inner.shape, BF16),
        vmem(twiddle.shape),
        vmem((3, 16, ch), BF16), vmem((3, seq + 8, ch)), vmem((3, seq, ch)),
        vmem((seq, ch)), vmem((seq, ch)), vmem((seq, ch)), vmem((seq, ch)),
        vmem((3, seq + 8, ch)),
        vmem((6, 16 * n, 2 * seq), BF16), vmem((6, 16 * n, 2 * seq), BF16),
        vmem((ch, d_cols), BF16), vmem((tokens4, d_cols), BF16),
        vmem((tokens4, max(ch, d_cols))), vmem((tokens4, ch), BF16),
        vmem((2, 2, seq, half), BF16), vmem((2, seq, half), BF16), vmem((2, seq, half), BF16),
        vmem((tokens4, ch), BF16),
        vmem((tokens4, d_cols), BF16), vmem((max(ny - 1, 1), tokens4, 256), BF16),
        vmem((tokens4, 128), BF16), vmem((tokens4, 128), BF16), vmem((tokens4, 128), BF16),
        vmem((2, q_rows, 2 * seq)), vmem((2, q_rows, 2 * seq)), vmem((2, q_rows, 2 * seq)),
        vmem((2 * n * GROUP, 2 * seq)),
        vmem((16, ch)), vmem((2, 8 * n, 128)), vmem((16, ch)),
        pltpu.SemaphoreType.DMA((4,)), pltpu.SemaphoreType.DMA((6,)), pltpu.SemaphoreType.DMA((7,)),
        pltpu.SemaphoreType.DMA((12,)), pltpu.SemaphoreType.DMA((12,)),
        pltpu.SemaphoreType.DMA((64,)), pltpu.SemaphoreType.DMA((64,)),
    ]
    shape = jax.ShapeDtypeStruct
    inside = pl.BlockSpec(memory_space=pltpu.VMEM)
    outside = pl.BlockSpec(memory_space=pl.ANY)
    out_shape = (
        shape(cot.shape, BF16),
        shape((seq, ch), BF16), shape((seq, ch), BF16), shape((seq, ch), BF16),
        shape((seq, ch), BF16),
        shape((1, ch), F32), shape((3, 3, ch), F32),
    )
    results = pl.pallas_call(
        lambda *refs: body(n, nz, ny, refs),
        out_shape=out_shape,
        in_specs=[outside] * 3 + [inside] * 3 + [outside, inside, outside, outside] + [outside] * 4,
        out_specs=[outside] * 7,
        scratch_shapes=scratch,
        compiler_params=pltpu.CompilerParams(
            collective_id=0, has_side_effects=True, vmem_limit_bytes=60 * 1024 * 1024
        ),
        name="hyena",
    )(query, key, value, tap_q, tap_k, tap_v, filt, skip.reshape(1, ch), weight, cot, *consts)
    results = pl.pallas_call(
        handover,
        out_shape=out_shape,
        in_specs=[outside] * 7,
        out_specs=[outside] * 7,
        scratch_shapes=[vmem(o.shape, o.dtype) for o in out_shape]
        + [pltpu.SemaphoreType.DMA((7,)), pltpu.SemaphoreType.DMA((7,))],
        name="handover",
    )(*results)
    return results[:5] + (results[5].reshape(ch), results[6])


def solution(mesh):
    in_specs = (
        P("ctx", "tp"),
        P("ctx", "tp"),
        P("ctx", "tp"),
        P(None, "tp"),
        P(None, "tp"),
        P(None, "tp"),
        P("ctx", "tp"),
        P("tp"),
        P("tp", "ctx"),
        P("ctx", "tp"),
    )
    out_specs = (
        P("ctx", "tp"),
        P("ctx", "tp"),
        P("ctx", "tp"),
        P("ctx", "tp"),
        P("ctx", "tp"),
        P("tp"),
        P(None, None, "tp"),
    )
    return jax.shard_map(local, mesh=mesh, in_specs=in_specs, out_specs=out_specs, check_vma=False)
```

```python
import jax
import jax.numpy as jnp
import ml_dtypes
import numpy as np
from jax import lax
from jax.experimental import pallas as pl
from jax.experimental.pallas import tpu as pltpu
from jax.sharding import PartitionSpec as P

F32 = jnp.float32
BF16 = jnp.bfloat16
GROUP = 16
FILTER, GATED, MIXING, GRAD_MIX, GRAD_GATED, GRAD_FILTER = range(6)
FILTER_PLACE, GATED_PLACE, ORDER, LATE_FILTER = 0, 3, 2, False
EARLY_FAR, SINGLE = False, True


def halves(matrix):
    high = matrix.astype(np.float32).astype(ml_dtypes.bfloat16)
    low = (matrix - high.astype(np.float64)).astype(np.float32).astype(ml_dtypes.bfloat16)
    return np.stack([high, low])


def tables(n, seq):
    total = 2 * n * seq
    q = np.arange(n + 1)
    m = np.arange(n)
    theta = 2 * np.pi * ((q[:, None] * m[None, :]) % (2 * n)) / (2 * n)
    forward = np.concatenate([np.cos(theta), -np.sin(theta)[1:n]])
    weight = np.where((q == 0) | (q == n), 1.0, 2.0)[:, None] / total
    back = np.concatenate([weight * np.cos(theta), (-weight * np.sin(theta))[1:n]]).T
    eye = np.eye(GROUP)
    j = np.arange(seq)
    phi = 2 * np.pi * ((j[:, None] * j[None, :]) % seq) / seq
    c, s = np.cos(phi), np.sin(phi)
    inner = np.block([[c, -s], [s, c]])
    inner_back = np.block([[c, s], [-s, c]])
    turn = 2 * np.pi * (q[:, None] * j[None, :]) / total
    twiddle = np.stack([np.cos(turn), np.sin(turn)]).astype(np.float32)
    twiddle = np.repeat(twiddle, GROUP, axis=1)
    return (
        halves(np.kron(forward, eye)),
        halves(np.kron(back, eye)),
        halves(np.stack([inner, inner_back])),
        twiddle,
    )


def split(value):
    high = value.astype(BF16)
    return high, (value - high.astype(F32)).astype(BF16)


def mm(left, right):
    return jnp.dot(left, right, preferred_element_type=F32)


def body(n, nz, ny, refs):
    (
        query_hbm, key_hbm, value_hbm, tap_q, tap_k, tap_v, filt_hbm, skip, weight, cot,
        outer_hbm, outer_back_hbm, inner_hbm, twiddle_hbm,
        mixed_hbm, grad_q_hbm, grad_k_hbm, grad_v_hbm, filter_hbm, skip_hbm, short_hbm,
        query, key, value, filt,
        mixed_out, out_grads, out_filter, out_skip, out_short,
        outer, outer_back, inner, twiddle,
        halo, ext, short, gated, mixing, grad_hidden, grad_mix, gext,
        sent, got, wide, cots, part, part_b, core_got, chip_sent, chip_got, hid,
        rows_b, rows_got, pair_sent, pair_got, final_b,
        spec_u, spec_h, spec_d, stage, tails, tails_got, tails_sum,
        const_sem, in_sem, out_sem, a2a_send, a2a_recv, send, recv,
    ) = refs
    seq, ch = query.shape
    half = ch // 2
    rows = 16 * n
    q_rows = GROUP * (n + 1)
    me = lax.axis_index("ctx")
    tp = lax.axis_index("tp")
    z, b = lax.div(me, 4), lax.rem(me, 4)
    xh, core = lax.div(b, 2), lax.rem(b, 2)
    y, xl = lax.div(tp, 2), lax.rem(tp, 2)
    counter = [0]
    pending = []

    def remote(src, dst, ctx, t):
        k = counter[0]
        counter[0] += 1
        copy = pltpu.make_async_remote_copy(
            src_ref=src, dst_ref=dst, send_sem=send.at[k], recv_sem=recv.at[k],
            device_id=(ctx, t), device_id_type=pl.DeviceIdType.MESH,
        )
        copy.start()
        pending.append(copy)
        return copy

    def at16(index):
        return pl.ds(pl.multiple_of(index * 16, 16), 16)

    def lanes(index, size=128):
        return pl.ds(pl.multiple_of(index * size, 128), size)

    def block(index, size=None):
        size = seq if size is None else size
        return pl.ds(pl.multiple_of(index * size, size), size)

    def peer(r):
        off = lax.div(r, 2)
        return lax.rem(me + n // 2 + off * (1 - 2 * lax.rem(r, 2)) + n, n)

    def spread(k, g=None):
        cols = pl.ds(0, 2 * seq) if g is None else pl.ds(g * seq, seq)
        sem = k if g is None else 8 + g

        def step(r, carry):
            dst = peer(r)
            pltpu.make_async_remote_copy(
                src_ref=sent.at[k, at16(dst), cols], dst_ref=got.at[k, at16(me), cols],
                send_sem=a2a_send.at[sem], recv_sem=a2a_recv.at[sem],
                device_id=(dst, tp), device_id_type=pl.DeviceIdType.MESH,
            ).start()
            return carry

        lax.fori_loop(1, n, step, 0)
        got[k, at16(me), cols] = sent[k, at16(me), cols]

    def arrive(k, g=None):
        cols = pl.ds(0, 2 * seq) if g is None else pl.ds(g * seq, seq)
        whole = got.at[k, pl.ds(0, rows - 16), cols]
        pltpu.make_async_copy(whole, whole, a2a_recv.at[k if g is None else 8 + g]).wait()

    def left(k, g=None):
        cols = pl.ds(0, 2 * seq) if g is None else pl.ds(g * seq, seq)
        whole = sent.at[k, pl.ds(0, rows - 16), cols]
        pltpu.make_async_copy(whole, whole, a2a_send.at[k if g is None else 8 + g]).wait()

    def half_to_channels(x, k, g):
        sent[k, :, g * seq : (g + 1) * seq] = x.T.astype(BF16)

    def to_channels(x, k):
        for g in range(2):
            half_to_channels(x[:, g * half : (g + 1) * half], k, g)

    def to_tokens(k):
        return jnp.concatenate(
            [got[k, :, g * seq : (g + 1) * seq].astype(F32).T for g in range(2)], axis=1
        )

    def forward(k, spec):
        u = got[k]
        stage[...] = mm(outer[0], u) + mm(outer[1], u)
        cos, sin = twiddle[0], twiddle[1]
        zero = jnp.zeros((GROUP, seq), F32)
        for g in range(2):
            cols = pl.ds(g * seq, seq)
            real = stage[:q_rows, cols]
            imag = jnp.concatenate([zero, stage[q_rows:, cols], zero])
            pair = jnp.concatenate([real * cos + imag * sin, imag * cos - real * sin], axis=1)
            high, low = split(pair)
            spec[g] = mm(high, inner[0, 0]) + mm(low, inner[0, 0]) + mm(high, inner[1, 0])

    def product(first, second, g, conj):
        ar, ai = first[g, :, :seq], first[g, :, seq:]
        br, bi = second[g, :, :seq], second[g, :, seq:]
        if conj:
            return jnp.concatenate([ar * br + ai * bi, ar * bi - ai * br], axis=1)
        return jnp.concatenate([ar * br - ai * bi, ar * bi + ai * br], axis=1)

    def inverse(first, second, conj, k):
        cos, sin = twiddle[0], twiddle[1]
        for g in range(2):
            high, low = split(product(first, second, g, conj))
            turned = mm(high, inner[0, 1]) + mm(low, inner[0, 1]) + mm(high, inner[1, 1])
            real, imag = turned[:, :seq], turned[:, seq:]
            cols = pl.ds(g * seq, seq)
            stage[:q_rows, cols] = real * cos - imag * sin
            stage[q_rows:, cols] = (imag * cos + real * sin)[GROUP : q_rows - GROUP]
        high, low = split(stage[...])
        result = mm(outer_back[0], high) + mm(outer_back[0], low) + mm(outer_back[1], high)
        sent[k] = result.astype(BF16)

    barrier = pltpu.get_barrier_semaphore()

    def greet(r, carry):
        pl.semaphore_signal(
            barrier, inc=1, device_id=(lax.rem(me + r, n), tp),
            device_id_type=pl.DeviceIdType.MESH,
        )
        return carry

    lax.fori_loop(1, n, greet, 0)
    others = [(y, 1 - xl)] + [(lax.rem(y + r, ny), xl) for r in range(1, ny)]
    for oy, ox in others:
        pl.semaphore_signal(
            barrier, inc=1, device_id=(me, oy * 2 + ox), device_id_type=pl.DeviceIdType.MESH
        )
    loads = [
        pltpu.make_async_copy(src, dst, in_sem.at[i])
        for i, (src, dst) in enumerate(
            [
                (filt_hbm, filt), (weight, wide.at[:, lanes(z)]),
                (cot.at[:, lanes(b)], cots.at[block(b), lanes(tp)]),
                (query_hbm, query), (key_hbm, key), (value_hbm, value),
            ]
        )
    ]
    for copy in loads:
        copy.start()
    consts = [
        pltpu.make_async_copy(src, dst, const_sem.at[i])
        for i, (src, dst) in enumerate(
            [(outer_hbm, outer), (inner_hbm, inner), (twiddle_hbm, twiddle), (outer_back_hbm, outer_back)]
        )
    ]
    for copy in consts:
        copy.start()
    pl.semaphore_wait(barrier, n - 1 + len(others))

    full = nz // 2 - 1
    up, down = lax.rem(z + 1, nz) * 4 + b, lax.rem(z + nz - 1, nz) * 4 + b

    def ring(s, c):
        piece = pl.ds(c * half, half)
        slot_up, slot_down = lanes(lax.rem(z + nz - s, nz)), lanes(lax.rem(z + s, nz))
        copies = []
        if s < full or c == 0:
            src = weight.at[piece] if s == 0 else wide.at[piece, slot_up]
            copies.append(remote(src, wide.at[piece, slot_up], up, tp))
        if s < full or c == 1:
            src = weight.at[piece] if s == 0 else wide.at[piece, slot_down]
            copies.append(remote(src, wide.at[piece, slot_down], down, tp))
        return copies

    def landed(copies):
        for copy in copies:
            copy.wait_recv()

    def mate(r):
        other = lax.rem(b + r, 4)
        return other, z * 4 + other

    hops = [ring(0, c) for c in range(2)]

    following, preceding = lax.rem(me + 1, n), lax.rem(me + n - 1, n)
    halos = [
        remote(x.at[pl.ds(seq - 16, 16)], halo.at[i], following, tp)
        for i, x in enumerate((query_hbm, key_hbm, value_hbm))
    ]

    def advance(s):
        for c in range(2):
            landed(hops[c])
            hops[c] = ring(s, c) if s <= full else []

    def send_at(place):
        if place == FILTER_PLACE:
            spread(FILTER)
        if place == GATED_PLACE:
            spread(GATED)

    cot_first = []
    for r in range(1, 4):
        other, ctx = mate(r)
        cot_first.append(remote(cot.at[:, lanes(other)], cots.at[block(b), lanes(tp)], ctx, tp))
    loads[0].wait()
    to_channels(filt[...], FILTER)
    send_at(0)

    tails[...] = jnp.zeros_like(tails)
    for copy in loads[1:]:
        copy.wait()
    landed(halos)
    taps = (tap_q, tap_k, tap_v)
    for i, x in enumerate((query, key, value)):
        ext[i, :8] = jnp.where(me == 0, 0.0, halo[i, 8:16].astype(F32))
        ext[i, 8:] = x[...].astype(F32)
        short[i] = (
            taps[i][0:1] * ext[i, pl.ds(8, seq)]
            + taps[i][1:2] * ext[i, pl.ds(7, seq)]
            + taps[i][2:3] * ext[i, pl.ds(6, seq)]
        )
    gated[...] = short[1] * short[2]
    to_channels(gated[...], GATED)

    landed(cot_first)
    cot_pair = remote(cots.at[:, lanes(tp)], cots.at[:, lanes(tp)], me, y * 2 + 1 - xl)
    send_at(1)
    for s in range(1, full):
        advance(s)
        send_at(1 + s)
        if s == 1:
            cot_pair.wait_recv()
            cot_last = [
                remote(cots.at[:, lanes(y, 256)], cots.at[:, lanes(y, 256)], me, oy * 2 + ox)
                for oy, ox in others[1:]
            ]
    if full < 2:
        cot_pair.wait_recv()
        cot_last = [
            remote(cots.at[:, lanes(y, 256)], cots.at[:, lanes(y, 256)], me, oy * 2 + ox)
            for oy, ox in others[1:]
        ]

    def slots(offsets):
        places = [lax.rem(z + nz + o, nz) for o in offsets]
        return (
            jnp.concatenate([cots[:, lanes(p)] for p in places], axis=1),
            lambda some: jnp.concatenate([wide[some, lanes(p)] for p in places], axis=1),
        )

    def add_slots(offsets, first):
        tokens, features = slots(offsets)
        for lo in range(0, ch, 256):
            some = pl.ds(lo, 256)
            term = lax.dot_general(
                tokens, features(some), (((1,), (1,)), ((), ())), preferred_element_type=F32
            )
            part[:, some] = term if first else part[:, some] + term

    if full > 0:
        advance(full)
    send_at(4)
    landed(cot_last)
    add_slots([0] + [o * w for o in range(1, full + 1) for w in (1, -1)], True)
    for copy in consts:
        copy.wait()
    if FILTER_PLACE < 2:
        arrive(FILTER)
        forward(FILTER, spec_h)

    advance(full + 1)
    sibling = z * 4 + xh * 2 + 1 - core
    twin = z * 4 + (1 - xh) * 2 + core
    far = (1 - xh) * 2 + core
    core_copies = []
    tokens, features = slots([full + 1])
    for g in range(2):
        cols = pl.ds(g * half, half)
        term = lax.dot_general(
            tokens, features(cols), (((1,), (1,)), ((), ())), preferred_element_type=F32
        )
        part[:, cols] += term
        for i in range(2):
            theirs = block(i * 2 + 1 - core)
            part_b[theirs, cols] = part[theirs, cols].astype(BF16)
        core_copies.append(
            [remote(part_b.at[block(i * 2 + 1 - core), cols], core_got.at[g, i], sibling, tp) for i in range(2)]
        )
    send_at(5)
    chip_copies = []
    for g in range(2):
        cols = pl.ds(g * half, half)
        landed(core_copies[g])
        chip_sent[g] = (part[block(far), cols] + core_got[g, 1 - xh].astype(F32)).astype(BF16)
        chip_copies.append(remote(chip_sent.at[g], chip_got.at[g], twin, tp))

    def mix(first, second):
        if first:
            arrive(GATED)
            forward(GATED, spec_u)
        if second:
            inverse(spec_h, spec_u, False, MIXING)
            spread(MIXING)

    if FILTER_PLACE >= 2 and ORDER != 0:
        arrive(FILTER)
        forward(FILTER, spec_h)
    mix(ORDER != 0, ORDER == 2)

    for g in range(2):
        cols = pl.ds(g * half, half)
        chip_copies[g].wait_recv()
        whole = part[block(b), cols] + core_got[g, xh].astype(F32) + chip_got[g].astype(F32)
        grad_hidden[:, cols] = whole
        whole = whole * short[0, :, cols]
        grad_mix[:, cols] = whole
        half_to_channels(whole, GRAD_MIX, g)
        if not SINGLE:
            spread(GRAD_MIX, g)
    if SINGLE:
        spread(GRAD_MIX)
    if FILTER_PLACE >= 2 and ORDER == 0:
        arrive(FILTER)
        forward(FILTER, spec_h)
    mix(ORDER == 0, ORDER != 2)
    tails[3, :] = jnp.sum(grad_mix[...] * gated[...], axis=0)

    hid_far = []

    def relay():
        for g in range(2):
            hid_twin[g].wait_recv()
            place = hid.at[block(far), pl.ds(g * half, half)]
            hid_far.append(remote(place, place, sibling, tp))

    def back():
        for g in (None,) if SINGLE else range(2):
            arrive(GRAD_MIX, g)
        forward(GRAD_MIX, spec_d)
        if EARLY_FAR:
            relay()
        inverse(spec_h, spec_d, True, GRAD_GATED)
        spread(GRAD_GATED)

    if ORDER != 2:
        back()

    arrive(MIXING)
    mixing[...] = to_tokens(MIXING) + skip[...] * gated[...]
    hid[block(b), :] = (short[0] * mixing[...]).astype(BF16)
    hid_sib = remote(hid.at[block(b)], hid.at[block(b)], sibling, tp)
    hid_twin = [
        remote(hid.at[block(b), pl.ds(g * half, half)], hid.at[block(b), pl.ds(g * half, half)], twin, tp)
        for g in range(2)
    ]
    gext[0, :seq] = grad_hidden[...] * mixing[...]
    halo_q = remote(gext.at[0, pl.ds(0, 8)], gext.at[0, pl.ds(seq, 8)], preceding, tp)

    def project(h):
        pair = block(h, 2 * seq)
        copies = []
        for r in list(range(1, ny)) + [0]:
            oy = lax.rem(y + r, ny)
            piece = mm(hid[pair, :], wide[:, lanes(oy, 256)])
            if r == 0:
                part[pair, lanes(oy, 256)] = piece
            else:
                rows_b[pair, lanes(oy, 256)] = piece.astype(BF16)
                copies.append(
                    remote(rows_b.at[pair, lanes(oy, 256)], rows_got.at[r - 1, pair], me, oy * 2 + xl)
                )
        return copies

    hid_sib.wait_recv()
    rows_near = project(xh)

    if ORDER == 2:
        back()

    if not EARLY_FAR:
        relay()
    else:
        landed(hid_far)
        rows_far = project(1 - xh)

    def hand_in(g):
        def step(r, carry):
            to_z = lax.rem(z + r, nz)
            dst = to_z * 4 + 3 - 3 * g

            @pl.when(dst != me)
            def _():
                pltpu.make_async_remote_copy(
                    src_ref=tails.at[pl.ds(8 * g, 8), lanes(to_z)], dst_ref=tails_got.at[g, block(me, 8)],
                    send_sem=a2a_send.at[6 + g], recv_sem=a2a_recv.at[6 + g],
                    device_id=(dst, tp), device_id_type=pl.DeviceIdType.MESH,
                ).start()

            return carry

        lax.fori_loop(0, nz, step, 0)
        tails_got[g, block(me, 8), :] = tails[8 * g : 8 * g + 8, lanes(z)]

    def tails_wait(sem, count):
        whole = tails_got.at[0, pl.ds(0, 8 * count)]
        pltpu.make_async_copy(whole, whole, sem).wait()

    def owner_wait(g, sem, count, other):
        owner = b == 3 - 3 * g

        @pl.when(owner)
        def _():
            tails_wait(sem, count)

        if other:
            @pl.when(jnp.logical_not(owner))
            def _():
                tails_wait(sem, other)

    def hand_out(g):
        place = tails_sum.at[pl.ds(8 * g, 8), lanes(z)]

        @pl.when(b == 3 - 3 * g)
        def _():
            tails_wait(a2a_recv.at[6 + g], n - 1)
            tails_sum[8 * g : 8 * g + 8, lanes(z)] = jnp.sum(tails_got[g].reshape(n, 8, 128), axis=0)

            def step(r, carry):
                pltpu.make_async_remote_copy(
                    src_ref=place, dst_ref=place,
                    send_sem=a2a_send.at[10 + g], recv_sem=a2a_recv.at[10 + g],
                    device_id=(peer(r), tp), device_id_type=pl.DeviceIdType.MESH,
                ).start()
                return carry

            lax.fori_loop(1, n, step, 0)

    def tap_sums(i):
        grads = gext[i, :seq]
        for o in range(3):
            tails[(0, 8, 11)[i] + o, :] = jnp.sum(grads * ext[i, pl.ds(8 - o, seq)], axis=0)

    tap_sums(0)
    hand_in(0)
    if not EARLY_FAR:
        landed(hid_far)
        rows_far = project(1 - xh)
    inverse(spec_u, spec_d, True, GRAD_FILTER)
    if not LATE_FILTER:
        spread(GRAD_FILTER)

    def collect(h, copies):
        pair = block(h, 2 * seq)
        landed(copies)
        for r in range(ny - 1):
            part[pair, lanes(y, 256)] += rows_got[r, pair].astype(F32)
        pair_sent[pair] = part[pair, lanes(y * 2 + 1 - xl)].astype(BF16)
        return remote(pair_sent.at[pair], pair_got.at[pair], me, y * 2 + 1 - xl)

    def finish(h, copy):
        pair = block(h, 2 * seq)
        copy.wait_recv()
        final_b[pair] = (part[pair, lanes(tp)] + pair_got[pair].astype(F32)).astype(BF16)

    def hand(other):
        return remote(final_b.at[block(other)], mixed_out.at[:, lanes(b)], z * 4 + other, tp)

    pair_near = collect(xh, rows_near)

    out_copies = []

    def store(src, dst):
        copy = pltpu.make_async_copy(src, dst, out_sem.at[len(out_copies)])
        copy.start()
        out_copies.append(copy)

    def returned(i, hbm):
        gext[i, seq:] = jnp.where(me == n - 1, 0.0, gext[i, seq:])
        out_grads[i] = (
            taps[i][0:1] * gext[i, pl.ds(0, seq)]
            + taps[i][1:2] * gext[i, pl.ds(1, seq)]
            + taps[i][2:3] * gext[i, pl.ds(2, seq)]
        ).astype(BF16)
        store(out_grads.at[i], hbm)

    halo_q.wait_recv()
    returned(0, grad_q_hbm)
    hand_out(0)

    arrive(GRAD_GATED)
    if LATE_FILTER:
        spread(GRAD_FILTER)
    grad = to_tokens(GRAD_GATED) + skip[...] * grad_mix[...]
    gext[1, :seq] = grad * short[2]
    gext[2, :seq] = grad * short[1]
    halo_kv = [
        remote(gext.at[i, pl.ds(0, 8)], gext.at[i, pl.ds(seq, 8)], preceding, tp) for i in (1, 2)
    ]
    tap_sums(1)
    tap_sums(2)

    hand_in(1)

    pair_far = collect(1 - xh, rows_far)
    finish(xh, pair_near)
    mixed_out[:, lanes(b)] = final_b[block(b), :]
    final_copies = [hand(xh * 2 + 1 - core)]

    hand_out(1)

    landed(halo_kv)
    returned(1, grad_k_hbm)
    returned(2, grad_v_hbm)
    finish(1 - xh, pair_far)
    final_copies += [hand(far), hand((1 - xh) * 2 + 1 - core)]
    arrive(GRAD_FILTER)
    out_filter[...] = to_tokens(GRAD_FILTER).astype(BF16)
    store(out_filter, filter_hbm)

    for g in range(2):
        owner_wait(g, a2a_recv.at[10 + g], nz - 1, nz)
    for i, row in enumerate((0, 8, 11)):
        out_short[i] = tails_sum[row : row + 3, :]
    out_skip[...] = tails_sum[3:4, :]
    store(out_short, short_hbm)
    store(out_skip, skip_hbm)
    landed(final_copies)
    store(mixed_out, mixed_hbm)
    for copy in pending:
        copy.wait_send()
    for k in (FILTER, GATED, MIXING, GRAD_GATED, GRAD_FILTER):
        left(k)
    for g in (None,) if SINGLE else range(2):
        left(GRAD_MIX, g)
    for g in range(2):
        owner_wait(g, a2a_send.at[6 + g], nz - 1, nz)
        owner_wait(g, a2a_send.at[10 + g], n - 1, 0)
    for copy in out_copies:
        copy.wait()


def handover(*refs):
    count = 7
    sources, targets, held = refs[:count], refs[count : 2 * count], refs[2 * count : 3 * count]
    in_sem, out_sem = refs[3 * count :]
    copies = [pltpu.make_async_copy(sources[i], held[i], in_sem.at[i]) for i in range(count)]
    for copy in copies:
        copy.start()
    outs = []
    for i in range(count):
        copies[i].wait()
        outs.append(pltpu.make_async_copy(held[i], targets[i], out_sem.at[i]))
        outs[-1].start()
    for copy in outs:
        copy.wait()


def local(*args):
    n, tp = lax.axis_size("ctx"), lax.axis_size("tp")
    nz, ny = n // 4, tp // 2
    query, key, value, tap_q, tap_k, tap_v, filt, skip, weight, cot = args
    seq, ch = query.shape
    consts = [jnp.asarray(t) for t in tables(n, seq)]
    outer, outer_back, inner, twiddle = consts
    q_rows = GROUP * (n + 1)
    d_cols = nz * 128
    tokens4 = 4 * seq
    half = ch // 2

    def vmem(shape, dtype=F32):
        return pltpu.VMEM(shape, dtype)

    scratch = [
        vmem((seq, ch), BF16), vmem((seq, ch), BF16), vmem((seq, ch), BF16), vmem((seq, ch)),
        vmem(cot.shape, BF16), vmem((3, seq, ch), BF16), vmem((seq, ch), BF16),
        vmem((1, ch)), vmem((3, 3, ch)),
        vmem(outer.shape, BF16), vmem(outer_back.shape, BF16), vmem(inner.shape, BF16),
        vmem(twiddle.shape),
        vmem((3, 16, ch), BF16), vmem((3, seq + 8, ch)), vmem((3, seq, ch)),
        vmem((seq, ch)), vmem((seq, ch)), vmem((seq, ch)), vmem((seq, ch)),
        vmem((3, seq + 8, ch)),
        vmem((6, 16 * n, 2 * seq), BF16), vmem((6, 16 * n, 2 * seq), BF16),
        vmem((ch, d_cols), BF16), vmem((tokens4, d_cols), BF16),
        vmem((tokens4, max(ch, d_cols))), vmem((tokens4, ch), BF16),
        vmem((2, 2, seq, half), BF16), vmem((2, seq, half), BF16), vmem((2, seq, half), BF16),
        vmem((tokens4, ch), BF16),
        vmem((tokens4, d_cols), BF16), vmem((max(ny - 1, 1), tokens4, 256), BF16),
        vmem((tokens4, 128), BF16), vmem((tokens4, 128), BF16), vmem((tokens4, 128), BF16),
        vmem((2, q_rows, 2 * seq)), vmem((2, q_rows, 2 * seq)), vmem((2, q_rows, 2 * seq)),
        vmem((2 * n * GROUP, 2 * seq)),
        vmem((16, ch)), vmem((2, 8 * n, 128)), vmem((16, ch)),
        pltpu.SemaphoreType.DMA((4,)), pltpu.SemaphoreType.DMA((6,)), pltpu.SemaphoreType.DMA((7,)),
        pltpu.SemaphoreType.DMA((12,)), pltpu.SemaphoreType.DMA((12,)),
        pltpu.SemaphoreType.DMA((64,)), pltpu.SemaphoreType.DMA((64,)),
    ]
    shape = jax.ShapeDtypeStruct
    inside = pl.BlockSpec(memory_space=pltpu.VMEM)
    outside = pl.BlockSpec(memory_space=pl.ANY)
    out_shape = (
        shape(cot.shape, BF16),
        shape((seq, ch), BF16), shape((seq, ch), BF16), shape((seq, ch), BF16),
        shape((seq, ch), BF16),
        shape((1, ch), F32), shape((3, 3, ch), F32),
    )
    results = pl.pallas_call(
        lambda *refs: body(n, nz, ny, refs),
        out_shape=out_shape,
        in_specs=[outside] * 3 + [inside] * 3 + [outside, inside, outside, outside] + [outside] * 4,
        out_specs=[outside] * 7,
        scratch_shapes=scratch,
        compiler_params=pltpu.CompilerParams(
            collective_id=0, has_side_effects=True, vmem_limit_bytes=60 * 1024 * 1024
        ),
        name="hyena",
    )(query, key, value, tap_q, tap_k, tap_v, filt, skip.reshape(1, ch), weight, cot, *consts)
    results = pl.pallas_call(
        handover,
        out_shape=out_shape,
        in_specs=[outside] * 7,
        out_specs=[outside] * 7,
        scratch_shapes=[vmem(o.shape, o.dtype) for o in out_shape]
        + [pltpu.SemaphoreType.DMA((7,)), pltpu.SemaphoreType.DMA((7,))],
        name="handover",
    )(*results)
    return results[:5] + (results[5].reshape(ch), results[6])


def solution(mesh):
    in_specs = (
        P("ctx", "tp"),
        P("ctx", "tp"),
        P("ctx", "tp"),
        P(None, "tp"),
        P(None, "tp"),
        P(None, "tp"),
        P("ctx", "tp"),
        P("tp"),
        P("tp", "ctx"),
        P("ctx", "tp"),
    )
    out_specs = (
        P("ctx", "tp"),
        P("ctx", "tp"),
        P("ctx", "tp"),
        P("ctx", "tp"),
        P("ctx", "tp"),
        P("tp"),
        P(None, None, "tp"),
    )
    return jax.shard_map(local, mesh=mesh, in_specs=in_specs, out_specs=out_specs, check_vma=False)
```

```python
import jax
import jax.numpy as jnp
import ml_dtypes
import numpy as np
from jax import lax
from jax.experimental import pallas as pl
from jax.experimental.pallas import tpu as pltpu
from jax.sharding import PartitionSpec as P

F32 = jnp.float32
BF16 = jnp.bfloat16
GROUP = 16
FILTER, GATED, MIXING, GRAD_MIX, GRAD_GATED, GRAD_FILTER = range(6)
FILTER_PLACE, GATED_PLACE, ORDER, LATE_FILTER = 0, 3, 2, False
EARLY_FAR, SINGLE = False, True


def halves(matrix):
    high = matrix.astype(np.float32).astype(ml_dtypes.bfloat16)
    low = (matrix - high.astype(np.float64)).astype(np.float32).astype(ml_dtypes.bfloat16)
    return np.stack([high, low])


def tables(n, seq):
    total = 2 * n * seq
    q = np.arange(n + 1)
    m = np.arange(n)
    theta = 2 * np.pi * ((q[:, None] * m[None, :]) % (2 * n)) / (2 * n)
    forward = np.concatenate([np.cos(theta), -np.sin(theta)[1:n]])
    weight = np.where((q == 0) | (q == n), 1.0, 2.0)[:, None] / total
    back = np.concatenate([weight * np.cos(theta), (-weight * np.sin(theta))[1:n]]).T
    eye = np.eye(GROUP)
    j = np.arange(seq)
    phi = 2 * np.pi * ((j[:, None] * j[None, :]) % seq) / seq
    c, s = np.cos(phi), np.sin(phi)
    inner = np.block([[c, -s], [s, c]])
    inner_back = np.block([[c, s], [-s, c]])
    turn = 2 * np.pi * (q[:, None] * j[None, :]) / total
    twiddle = np.stack([np.cos(turn), np.sin(turn)]).astype(np.float32)
    twiddle = np.repeat(twiddle, GROUP, axis=1)
    return (
        halves(np.kron(forward, eye)),
        halves(np.kron(back, eye)),
        halves(np.stack([inner, inner_back])),
        twiddle,
    )


def split(value):
    high = value.astype(BF16)
    return high, (value - high.astype(F32)).astype(BF16)


def mm(left, right):
    return jnp.dot(left, right, preferred_element_type=F32)


def body(n, nz, ny, refs):
    (
        query_hbm, key_hbm, value_hbm, tap_q, tap_k, tap_v, filt_hbm, skip, weight, cot,
        outer_hbm, outer_back_hbm, inner_hbm, twiddle_hbm,
        mixed_hbm, grad_q_hbm, grad_k_hbm, grad_v_hbm, filter_hbm, skip_hbm, short_hbm,
        query, key, value, filt,
        mixed_out, out_grads, out_filter, out_skip, out_short,
        outer, outer_back, inner, twiddle,
        halo, ext, short, gated, mixing, grad_hidden, grad_mix, gext,
        sent, got, wide, cots, part, part_b, core_got, chip_sent, chip_got, hid,
        rows_b, rows_got, pair_sent, pair_got, final_b,
        spec_u, spec_h, spec_d, stage, tails, tails_got, tails_sum,
        const_sem, in_sem, out_sem, a2a_send, a2a_recv, send, recv,
    ) = refs
    seq, ch = query.shape
    half = ch // 2
    rows = 16 * n
    q_rows = GROUP * (n + 1)
    me = lax.axis_index("ctx")
    tp = lax.axis_index("tp")
    z, b = lax.div(me, 4), lax.rem(me, 4)
    xh, core = lax.div(b, 2), lax.rem(b, 2)
    y, xl = lax.div(tp, 2), lax.rem(tp, 2)
    counter = [0]
    pending = []

    def remote(src, dst, ctx, t):
        k = counter[0]
        counter[0] += 1
        copy = pltpu.make_async_remote_copy(
            src_ref=src, dst_ref=dst, send_sem=send.at[k], recv_sem=recv.at[k],
            device_id=(ctx, t), device_id_type=pl.DeviceIdType.MESH,
        )
        copy.start()
        pending.append(copy)
        return copy

    def at16(index):
        return pl.ds(pl.multiple_of(index * 16, 16), 16)

    def lanes(index, size=128):
        return pl.ds(pl.multiple_of(index * size, 128), size)

    def block(index, size=None):
        size = seq if size is None else size
        return pl.ds(pl.multiple_of(index * size, size), size)

    def peer(r):
        off = lax.div(r, 2)
        return lax.rem(me + n // 2 + off * (1 - 2 * lax.rem(r, 2)) + n, n)

    def spread(k, g=None):
        cols = pl.ds(0, 2 * seq) if g is None else pl.ds(g * seq, seq)
        sem = k if g is None else 8 + g

        def step(r, carry):
            dst = peer(r)
            pltpu.make_async_remote_copy(
                src_ref=sent.at[k, at16(dst), cols], dst_ref=got.at[k, at16(me), cols],
                send_sem=a2a_send.at[sem], recv_sem=a2a_recv.at[sem],
                device_id=(dst, tp), device_id_type=pl.DeviceIdType.MESH,
            ).start()
            return carry

        lax.fori_loop(1, n, step, 0)
        got[k, at16(me), cols] = sent[k, at16(me), cols]

    def arrive(k, g=None):
        cols = pl.ds(0, 2 * seq) if g is None else pl.ds(g * seq, seq)
        whole = got.at[k, pl.ds(0, rows - 16), cols]
        pltpu.make_async_copy(whole, whole, a2a_recv.at[k if g is None else 8 + g]).wait()

    def left(k, g=None):
        cols = pl.ds(0, 2 * seq) if g is None else pl.ds(g * seq, seq)
        whole = sent.at[k, pl.ds(0, rows - 16), cols]
        pltpu.make_async_copy(whole, whole, a2a_send.at[k if g is None else 8 + g]).wait()

    def half_to_channels(x, k, g):
        sent[k, :, g * seq : (g + 1) * seq] = x.T.astype(BF16)

    def to_channels(x, k):
        for g in range(2):
            half_to_channels(x[:, g * half : (g + 1) * half], k, g)

    def to_tokens(k):
        return jnp.concatenate(
            [got[k, :, g * seq : (g + 1) * seq].astype(F32).T for g in range(2)], axis=1
        )

    def forward(k, spec):
        u = got[k]
        stage[...] = mm(outer[0], u) + mm(outer[1], u)
        cos, sin = twiddle[0], twiddle[1]
        zero = jnp.zeros((GROUP, seq), F32)
        for g in range(2):
            cols = pl.ds(g * seq, seq)
            real = stage[:q_rows, cols]
            imag = jnp.concatenate([zero, stage[q_rows:, cols], zero])
            pair = jnp.concatenate([real * cos + imag * sin, imag * cos - real * sin], axis=1)
            high, low = split(pair)
            spec[g] = mm(high, inner[0, 0]) + mm(low, inner[0, 0]) + mm(high, inner[1, 0])

    def product(first, second, g, conj):
        ar, ai = first[g, :, :seq], first[g, :, seq:]
        br, bi = second[g, :, :seq], second[g, :, seq:]
        if conj:
            return jnp.concatenate([ar * br + ai * bi, ar * bi - ai * br], axis=1)
        return jnp.concatenate([ar * br - ai * bi, ar * bi + ai * br], axis=1)

    def inverse(first, second, conj, k):
        cos, sin = twiddle[0], twiddle[1]
        for g in range(2):
            high, low = split(product(first, second, g, conj))
            turned = mm(high, inner[0, 1]) + mm(low, inner[0, 1]) + mm(high, inner[1, 1])
            real, imag = turned[:, :seq], turned[:, seq:]
            cols = pl.ds(g * seq, seq)
            stage[:q_rows, cols] = real * cos - imag * sin
            stage[q_rows:, cols] = (imag * cos + real * sin)[GROUP : q_rows - GROUP]
        high, low = split(stage[...])
        result = mm(outer_back[0], high) + mm(outer_back[0], low) + mm(outer_back[1], high)
        sent[k] = result.astype(BF16)

    barrier = pltpu.get_barrier_semaphore()

    def greet(r, carry):
        pl.semaphore_signal(
            barrier, inc=1, device_id=(lax.rem(me + r, n), tp),
            device_id_type=pl.DeviceIdType.MESH,
        )
        return carry

    lax.fori_loop(1, n, greet, 0)
    others = [(y, 1 - xl)] + [(lax.rem(y + r, ny), xl) for r in range(1, ny)]
    for oy, ox in others:
        pl.semaphore_signal(
            barrier, inc=1, device_id=(me, oy * 2 + ox), device_id_type=pl.DeviceIdType.MESH
        )
    loads = [
        pltpu.make_async_copy(src, dst, in_sem.at[i])
        for i, (src, dst) in enumerate(
            [
                (filt_hbm, filt), (weight, wide.at[:, lanes(z)]),
                (cot.at[:, lanes(b)], cots.at[block(b), lanes(tp)]),
                (query_hbm, query), (key_hbm, key), (value_hbm, value),
            ]
        )
    ]
    for copy in loads:
        copy.start()
    consts = [
        pltpu.make_async_copy(src, dst, const_sem.at[i])
        for i, (src, dst) in enumerate(
            [(outer_hbm, outer), (inner_hbm, inner), (twiddle_hbm, twiddle), (outer_back_hbm, outer_back)]
        )
    ]
    for copy in consts:
        copy.start()
    pl.semaphore_wait(barrier, n - 1 + len(others))

    quarter = ch // 4
    full = nz // 2 - 1
    up, down = lax.rem(z + 1, nz) * 4 + b, lax.rem(z + nz - 1, nz) * 4 + b

    def ring(s, c):
        piece = pl.ds(c * quarter, quarter)
        slot_up, slot_down = lanes(lax.rem(z + nz - s, nz)), lanes(lax.rem(z + s, nz))
        copies = []
        if s < full or c < 2:
            src = weight.at[piece] if s == 0 else wide.at[piece, slot_up]
            copies.append(remote(src, wide.at[piece, slot_up], up, tp))
        if s < full or c >= 2:
            src = weight.at[piece] if s == 0 else wide.at[piece, slot_down]
            copies.append(remote(src, wide.at[piece, slot_down], down, tp))
        return copies

    def landed(copies):
        for copy in copies:
            copy.wait_recv()

    def mate(r):
        other = lax.rem(b + r, 4)
        return other, z * 4 + other

    hops = [ring(0, c) for c in range(4)]

    following, preceding = lax.rem(me + 1, n), lax.rem(me + n - 1, n)
    halos = [
        remote(x.at[pl.ds(seq - 16, 16)], halo.at[i], following, tp)
        for i, x in enumerate((query_hbm, key_hbm, value_hbm))
    ]

    def advance(s):
        for c in range(4):
            landed(hops[c])
            hops[c] = ring(s, c) if s <= full else []

    def send_at(place):
        if place == FILTER_PLACE:
            spread(FILTER)
        if place == GATED_PLACE:
            spread(GATED)

    cot_first = []
    for r in range(1, 4):
        other, ctx = mate(r)
        cot_first.append(remote(cot.at[:, lanes(other)], cots.at[block(b), lanes(tp)], ctx, tp))
    loads[0].wait()
    to_channels(filt[...], FILTER)
    send_at(0)

    tails[...] = jnp.zeros_like(tails)
    for copy in loads[1:]:
        copy.wait()
    landed(halos)
    taps = (tap_q, tap_k, tap_v)
    for i, x in enumerate((query, key, value)):
        ext[i, :8] = jnp.where(me == 0, 0.0, halo[i, 8:16].astype(F32))
        ext[i, 8:] = x[...].astype(F32)
        short[i] = (
            taps[i][0:1] * ext[i, pl.ds(8, seq)]
            + taps[i][1:2] * ext[i, pl.ds(7, seq)]
            + taps[i][2:3] * ext[i, pl.ds(6, seq)]
        )
    gated[...] = short[1] * short[2]
    to_channels(gated[...], GATED)

    landed(cot_first)
    cot_pair = remote(cots.at[:, lanes(tp)], cots.at[:, lanes(tp)], me, y * 2 + 1 - xl)
    send_at(1)
    for s in range(1, full):
        advance(s)
        send_at(1 + s)
        if s == 1:
            cot_pair.wait_recv()
            cot_last = [
                remote(cots.at[:, lanes(y, 256)], cots.at[:, lanes(y, 256)], me, oy * 2 + ox)
                for oy, ox in others[1:]
            ]
    if full < 2:
        cot_pair.wait_recv()
        cot_last = [
            remote(cots.at[:, lanes(y, 256)], cots.at[:, lanes(y, 256)], me, oy * 2 + ox)
            for oy, ox in others[1:]
        ]

    def slots(offsets):
        places = [lax.rem(z + nz + o, nz) for o in offsets]
        return (
            jnp.concatenate([cots[:, lanes(p)] for p in places], axis=1),
            lambda some: jnp.concatenate([wide[some, lanes(p)] for p in places], axis=1),
        )

    def add_slots(offsets, first):
        tokens, features = slots(offsets)
        for lo in range(0, ch, 256):
            some = pl.ds(lo, 256)
            term = lax.dot_general(
                tokens, features(some), (((1,), (1,)), ((), ())), preferred_element_type=F32
            )
            part[:, some] = term if first else part[:, some] + term

    if full > 0:
        advance(full)
    send_at(4)
    landed(cot_last)
    add_slots([0] + [o * w for o in range(1, full + 1) for w in (1, -1)], True)
    for copy in consts:
        copy.wait()
    if FILTER_PLACE < 2:
        arrive(FILTER)
        forward(FILTER, spec_h)

    advance(full + 1)
    sibling = z * 4 + xh * 2 + 1 - core
    twin = z * 4 + (1 - xh) * 2 + core
    far = (1 - xh) * 2 + core
    core_copies = []
    tokens, features = slots([full + 1])
    for g in range(2):
        cols = pl.ds(g * half, half)
        term = lax.dot_general(
            tokens, features(cols), (((1,), (1,)), ((), ())), preferred_element_type=F32
        )
        part[:, cols] += term
        for i in range(2):
            theirs = block(i * 2 + 1 - core)
            part_b[theirs, cols] = part[theirs, cols].astype(BF16)
        core_copies.append(
            [remote(part_b.at[block(i * 2 + 1 - core), cols], core_got.at[g, i], sibling, tp) for i in range(2)]
        )
    send_at(5)
    chip_copies = []
    for g in range(2):
        cols = pl.ds(g * half, half)
        landed(core_copies[g])
        chip_sent[g] = (part[block(far), cols] + core_got[g, 1 - xh].astype(F32)).astype(BF16)
        chip_copies.append(remote(chip_sent.at[g], chip_got.at[g], twin, tp))

    def mix(first, second):
        if first:
            arrive(GATED)
            forward(GATED, spec_u)
        if second:
            inverse(spec_h, spec_u, False, MIXING)
            spread(MIXING)

    if FILTER_PLACE >= 2 and ORDER != 0:
        arrive(FILTER)
        forward(FILTER, spec_h)
    mix(ORDER != 0, ORDER == 2)

    for g in range(2):
        cols = pl.ds(g * half, half)
        chip_copies[g].wait_recv()
        whole = part[block(b), cols] + core_got[g, xh].astype(F32) + chip_got[g].astype(F32)
        grad_hidden[:, cols] = whole
        whole = whole * short[0, :, cols]
        grad_mix[:, cols] = whole
        half_to_channels(whole, GRAD_MIX, g)
        if not SINGLE:
            spread(GRAD_MIX, g)
    if SINGLE:
        spread(GRAD_MIX)
    if FILTER_PLACE >= 2 and ORDER == 0:
        arrive(FILTER)
        forward(FILTER, spec_h)
    mix(ORDER == 0, ORDER != 2)
    tails[3, :] = jnp.sum(grad_mix[...] * gated[...], axis=0)

    hid_far = []

    def relay():
        for g in range(2):
            hid_twin[g].wait_recv()
            place = hid.at[block(far), pl.ds(g * half, half)]
            hid_far.append(remote(place, place, sibling, tp))

    def back():
        for g in (None,) if SINGLE else range(2):
            arrive(GRAD_MIX, g)
        forward(GRAD_MIX, spec_d)
        if EARLY_FAR:
            relay()
        inverse(spec_h, spec_d, True, GRAD_GATED)
        spread(GRAD_GATED)

    if ORDER != 2:
        back()

    arrive(MIXING)
    mixing[...] = to_tokens(MIXING) + skip[...] * gated[...]
    hid[block(b), :] = (short[0] * mixing[...]).astype(BF16)
    hid_sib = remote(hid.at[block(b)], hid.at[block(b)], sibling, tp)
    hid_twin = [
        remote(hid.at[block(b), pl.ds(g * half, half)], hid.at[block(b), pl.ds(g * half, half)], twin, tp)
        for g in range(2)
    ]
    gext[0, :seq] = grad_hidden[...] * mixing[...]
    halo_q = remote(gext.at[0, pl.ds(0, 8)], gext.at[0, pl.ds(seq, 8)], preceding, tp)

    def project(h):
        pair = block(h, 2 * seq)
        copies = []
        for r in list(range(1, ny)) + [0]:
            oy = lax.rem(y + r, ny)
            piece = mm(hid[pair, :], wide[:, lanes(oy, 256)])
            if r == 0:
                part[pair, lanes(oy, 256)] = piece
            else:
                rows_b[pair, lanes(oy, 256)] = piece.astype(BF16)
                copies.append(
                    remote(rows_b.at[pair, lanes(oy, 256)], rows_got.at[r - 1, pair], me, oy * 2 + xl)
                )
        return copies

    hid_sib.wait_recv()
    rows_near = project(xh)

    if ORDER == 2:
        back()

    if not EARLY_FAR:
        relay()
    else:
        landed(hid_far)
        rows_far = project(1 - xh)

    def hand_in(g):
        def step(r, carry):
            to_z = lax.rem(z + r, nz)
            dst = to_z * 4 + 3 - 3 * g

            @pl.when(dst != me)
            def _():
                pltpu.make_async_remote_copy(
                    src_ref=tails.at[pl.ds(8 * g, 8), lanes(to_z)], dst_ref=tails_got.at[g, block(me, 8)],
                    send_sem=a2a_send.at[6 + g], recv_sem=a2a_recv.at[6 + g],
                    device_id=(dst, tp), device_id_type=pl.DeviceIdType.MESH,
                ).start()

            return carry

        lax.fori_loop(0, nz, step, 0)
        tails_got[g, block(me, 8), :] = tails[8 * g : 8 * g + 8, lanes(z)]

    def tails_wait(sem, count):
        whole = tails_got.at[0, pl.ds(0, 8 * count)]
        pltpu.make_async_copy(whole, whole, sem).wait()

    def owner_wait(g, sem, count, other):
        owner = b == 3 - 3 * g

        @pl.when(owner)
        def _():
            tails_wait(sem, count)

        if other:
            @pl.when(jnp.logical_not(owner))
            def _():
                tails_wait(sem, other)

    def hand_out(g):
        place = tails_sum.at[pl.ds(8 * g, 8), lanes(z)]

        @pl.when(b == 3 - 3 * g)
        def _():
            tails_wait(a2a_recv.at[6 + g], n - 1)
            tails_sum[8 * g : 8 * g + 8, lanes(z)] = jnp.sum(tails_got[g].reshape(n, 8, 128), axis=0)

            def step(r, carry):
                pltpu.make_async_remote_copy(
                    src_ref=place, dst_ref=place,
                    send_sem=a2a_send.at[10 + g], recv_sem=a2a_recv.at[10 + g],
                    device_id=(peer(r), tp), device_id_type=pl.DeviceIdType.MESH,
                ).start()
                return carry

            lax.fori_loop(1, n, step, 0)

    def tap_sums(i):
        grads = gext[i, :seq]
        for o in range(3):
            tails[(0, 8, 11)[i] + o, :] = jnp.sum(grads * ext[i, pl.ds(8 - o, seq)], axis=0)

    tap_sums(0)
    hand_in(0)
    inverse(spec_u, spec_d, True, GRAD_FILTER)
    if not EARLY_FAR:
        landed(hid_far)
        rows_far = project(1 - xh)
    if not LATE_FILTER:
        spread(GRAD_FILTER)

    def collect(h, copies):
        pair = block(h, 2 * seq)
        landed(copies)
        for r in range(ny - 1):
            part[pair, lanes(y, 256)] += rows_got[r, pair].astype(F32)
        pair_sent[pair] = part[pair, lanes(y * 2 + 1 - xl)].astype(BF16)
        return remote(pair_sent.at[pair], pair_got.at[pair], me, y * 2 + 1 - xl)

    def finish(h, copy):
        pair = block(h, 2 * seq)
        copy.wait_recv()
        final_b[pair] = (part[pair, lanes(tp)] + pair_got[pair].astype(F32)).astype(BF16)

    def hand(other):
        return remote(final_b.at[block(other)], mixed_out.at[:, lanes(b)], z * 4 + other, tp)

    pair_near = collect(xh, rows_near)

    out_copies = []

    def store(src, dst):
        copy = pltpu.make_async_copy(src, dst, out_sem.at[len(out_copies)])
        copy.start()
        out_copies.append(copy)

    def returned(i, hbm):
        gext[i, seq:] = jnp.where(me == n - 1, 0.0, gext[i, seq:])
        out_grads[i] = (
            taps[i][0:1] * gext[i, pl.ds(0, seq)]
            + taps[i][1:2] * gext[i, pl.ds(1, seq)]
            + taps[i][2:3] * gext[i, pl.ds(2, seq)]
        ).astype(BF16)
        store(out_grads.at[i], hbm)

    halo_q.wait_recv()
    returned(0, grad_q_hbm)
    hand_out(0)

    arrive(GRAD_GATED)
    if LATE_FILTER:
        spread(GRAD_FILTER)
    grad = to_tokens(GRAD_GATED) + skip[...] * grad_mix[...]
    gext[1, :seq] = grad * short[2]
    gext[2, :seq] = grad * short[1]
    halo_kv = [
        remote(gext.at[i, pl.ds(0, 8)], gext.at[i, pl.ds(seq, 8)], preceding, tp) for i in (1, 2)
    ]
    tap_sums(1)
    tap_sums(2)

    hand_in(1)

    pair_far = collect(1 - xh, rows_far)
    finish(xh, pair_near)
    mixed_out[:, lanes(b)] = final_b[block(b), :]
    final_copies = [hand(xh * 2 + 1 - core)]

    hand_out(1)

    landed(halo_kv)
    returned(1, grad_k_hbm)
    returned(2, grad_v_hbm)
    finish(1 - xh, pair_far)
    final_copies += [hand(far), hand((1 - xh) * 2 + 1 - core)]
    arrive(GRAD_FILTER)
    out_filter[...] = to_tokens(GRAD_FILTER).astype(BF16)
    store(out_filter, filter_hbm)

    for g in range(2):
        owner_wait(g, a2a_recv.at[10 + g], nz - 1, nz)
    for i, row in enumerate((0, 8, 11)):
        out_short[i] = tails_sum[row : row + 3, :]
    out_skip[...] = tails_sum[3:4, :]
    store(out_short, short_hbm)
    store(out_skip, skip_hbm)
    landed(final_copies)
    store(mixed_out, mixed_hbm)
    for copy in pending:
        copy.wait_send()
    for k in (FILTER, GATED, MIXING, GRAD_GATED, GRAD_FILTER):
        left(k)
    for g in (None,) if SINGLE else range(2):
        left(GRAD_MIX, g)
    for g in range(2):
        owner_wait(g, a2a_send.at[6 + g], nz - 1, nz)
        owner_wait(g, a2a_send.at[10 + g], n - 1, 0)
    for copy in out_copies:
        copy.wait()


def handover(*refs):
    count = 7
    sources, targets, held = refs[:count], refs[count : 2 * count], refs[2 * count : 3 * count]
    in_sem, out_sem = refs[3 * count :]
    copies = [pltpu.make_async_copy(sources[i], held[i], in_sem.at[i]) for i in range(count)]
    for copy in copies:
        copy.start()
    outs = []
    for i in range(count):
        copies[i].wait()
        outs.append(pltpu.make_async_copy(held[i], targets[i], out_sem.at[i]))
        outs[-1].start()
    for copy in outs:
        copy.wait()


def local(*args):
    n, tp = lax.axis_size("ctx"), lax.axis_size("tp")
    nz, ny = n // 4, tp // 2
    query, key, value, tap_q, tap_k, tap_v, filt, skip, weight, cot = args
    seq, ch = query.shape
    consts = [jnp.asarray(t) for t in tables(n, seq)]
    outer, outer_back, inner, twiddle = consts
    q_rows = GROUP * (n + 1)
    d_cols = nz * 128
    tokens4 = 4 * seq
    half = ch // 2

    def vmem(shape, dtype=F32):
        return pltpu.VMEM(shape, dtype)

    scratch = [
        vmem((seq, ch), BF16), vmem((seq, ch), BF16), vmem((seq, ch), BF16), vmem((seq, ch)),
        vmem(cot.shape, BF16), vmem((3, seq, ch), BF16), vmem((seq, ch), BF16),
        vmem((1, ch)), vmem((3, 3, ch)),
        vmem(outer.shape, BF16), vmem(outer_back.shape, BF16), vmem(inner.shape, BF16),
        vmem(twiddle.shape),
        vmem((3, 16, ch), BF16), vmem((3, seq + 8, ch)), vmem((3, seq, ch)),
        vmem((seq, ch)), vmem((seq, ch)), vmem((seq, ch)), vmem((seq, ch)),
        vmem((3, seq + 8, ch)),
        vmem((6, 16 * n, 2 * seq), BF16), vmem((6, 16 * n, 2 * seq), BF16),
        vmem((ch, d_cols), BF16), vmem((tokens4, d_cols), BF16),
        vmem((tokens4, max(ch, d_cols))), vmem((tokens4, ch), BF16),
        vmem((2, 2, seq, half), BF16), vmem((2, seq, half), BF16), vmem((2, seq, half), BF16),
        vmem((tokens4, ch), BF16),
        vmem((tokens4, d_cols), BF16), vmem((max(ny - 1, 1), tokens4, 256), BF16),
        vmem((tokens4, 128), BF16), vmem((tokens4, 128), BF16), vmem((tokens4, 128), BF16),
        vmem((2, q_rows, 2 * seq)), vmem((2, q_rows, 2 * seq)), vmem((2, q_rows, 2 * seq)),
        vmem((2 * n * GROUP, 2 * seq)),
        vmem((16, ch)), vmem((2, 8 * n, 128)), vmem((16, ch)),
        pltpu.SemaphoreType.DMA((4,)), pltpu.SemaphoreType.DMA((6,)), pltpu.SemaphoreType.DMA((7,)),
        pltpu.SemaphoreType.DMA((12,)), pltpu.SemaphoreType.DMA((12,)),
        pltpu.SemaphoreType.DMA((72,)), pltpu.SemaphoreType.DMA((72,)),
    ]
    shape = jax.ShapeDtypeStruct
    inside = pl.BlockSpec(memory_space=pltpu.VMEM)
    outside = pl.BlockSpec(memory_space=pl.ANY)
    out_shape = (
        shape(cot.shape, BF16),
        shape((seq, ch), BF16), shape((seq, ch), BF16), shape((seq, ch), BF16),
        shape((seq, ch), BF16),
        shape((1, ch), F32), shape((3, 3, ch), F32),
    )
    results = pl.pallas_call(
        lambda *refs: body(n, nz, ny, refs),
        out_shape=out_shape,
        in_specs=[outside] * 3 + [inside] * 3 + [outside, inside, outside, outside] + [outside] * 4,
        out_specs=[outside] * 7,
        scratch_shapes=scratch,
        compiler_params=pltpu.CompilerParams(
            collective_id=0, has_side_effects=True, vmem_limit_bytes=60 * 1024 * 1024
        ),
        name="hyena",
    )(query, key, value, tap_q, tap_k, tap_v, filt, skip.reshape(1, ch), weight, cot, *consts)
    results = pl.pallas_call(
        handover,
        out_shape=out_shape,
        in_specs=[outside] * 7,
        out_specs=[outside] * 7,
        scratch_shapes=[vmem(o.shape, o.dtype) for o in out_shape]
        + [pltpu.SemaphoreType.DMA((7,)), pltpu.SemaphoreType.DMA((7,))],
        name="handover",
    )(*results)
    return results[:5] + (results[5].reshape(ch), results[6])


def solution(mesh):
    in_specs = (
        P("ctx", "tp"),
        P("ctx", "tp"),
        P("ctx", "tp"),
        P(None, "tp"),
        P(None, "tp"),
        P(None, "tp"),
        P("ctx", "tp"),
        P("tp"),
        P("tp", "ctx"),
        P("ctx", "tp"),
    )
    out_specs = (
        P("ctx", "tp"),
        P("ctx", "tp"),
        P("ctx", "tp"),
        P("ctx", "tp"),
        P("ctx", "tp"),
        P("tp"),
        P(None, None, "tp"),
    )
    return jax.shard_map(local, mesh=mesh, in_specs=in_specs, out_specs=out_specs, check_vma=False)
```
